512 devices in a mesh: span: 64 (over y, z), chord: 8 (over x, core).
Axes of the slice: x: 4, y: 4, z: 16, core: 2. Of those that a mesh axis runs over, the one named last changes fastest.
Arguments:
- schur: bfloat16 [64, 8, 1536, 1536], P('span', 'chord'), may hold values from -1 to 5, as said below
- loads: bfloat16 [64, 8, 64, 1536], P('span', 'chord'), may hold values from -24 to 24
- interface_rows: int32 [64, 8, 4, 384], P('span', 'chord'), may hold values from 0 to 1535, as said below
- edge_rows: int32 [64, 8, 4], P('span', 'chord'), may hold values from 0 to 384, as said below
- corner_rows: int32 [64, 8, 128], P('span', 'chord'), may hold values from 0 to 1535, as said below
- corner_map: int32 [64, 8, 128], P('span', 'chord'), may hold values from 0 to 383
- coarse_inverse: float32 [64, 384, 384], P('span', 'chord'), may hold values from -1 to 2, as said below
Outputs:
- solution: bfloat16 [64, 8, 64, 1536], P('span', 'chord')
The draws below stay inside these ranges and needn't reach their ends.
Inputs may be any that keep to these rules, and one draw needn't show every extreme that they name: `schur`: each subdomain's matrix is symmetric positive definite. `interface_rows`: the 1536 entries of one subdomain are distinct. `edge_rows`: entry d is the number of live rows shared with the neighbour on side d; it equals that neighbour's entry for the opposite side, is 0 exactly where side d lies outside the grid, and some pairs of neighbours share all 384 rows. `corner_rows`: the 128 entries of one subdomain are distinct. `coarse_inverse`: each span index's matrix is symmetric positive definite.
All inputs are finite; a program needn't handle non-finite values.
Results may differ from the reference program's by a relative error of at most 0.0029.
Values may be sent and summed in bfloat16 or wider, within the bound.
No kernel may reach another device: no remote copies, remote signals or barrier semaphores. Data moves between devices by JAX's collectives and lax.ppermute only.
A program may use at most 64 MiB of HBM per device.

```python
import jax
import jax.numpy as jnp
from jax import lax

M = 1536
K = 384
CASES = 64
NCORN = 128
ITERS = 5
CROWS = 384
N_SPAN = 64
N_CHORD = 8


def draw_schur(key, part):
    key = jax.random.fold_in(key, 11)

    def one_span(index):
        local_key = jax.random.fold_in(key, index)
        first, second = jax.random.split(local_key)
        raw = jnp.clip(jax.random.normal(first, (N_CHORD, M, M), jnp.float32), -4.0, 4.0)
        raw = raw * (0.5 / jnp.sqrt(jnp.float32(M)))
        off = (raw + jnp.swapaxes(raw, 1, 2)) * 0.70710678
        diag = jax.random.uniform(second, (N_CHORD, M), jnp.float32, 2.5, 5.0)
        eye = jnp.eye(M, dtype=jnp.float32)
        return (off * (1.0 - eye) + diag[:, :, None] * eye).astype(jnp.bfloat16)
    return lax.map(one_span, jnp.arange(N_SPAN, dtype=jnp.int32))


def draw_loads(key, part):
    key = jax.random.fold_in(key, 12)
    first = jax.random.fold_in(key, 0)
    rise = 3.0 ** (jnp.arange(N_SPAN, dtype=jnp.float32) / max(N_SPAN - 1, 1))
    values = jnp.clip(jax.random.normal(first, (N_SPAN, N_CHORD, CASES, M), jnp.float32), -4.0, 4.0)
    return (values * rise[:, None, None, None]).astype(jnp.bfloat16)


def draw_interface_rows(key, part):
    key = jax.random.fold_in(key, 13)
    keys = jax.random.split(key, N_SPAN * N_CHORD)
    orders = jax.vmap(lambda single: jax.random.permutation(single, M))(keys)
    return orders[:, :4 * K].reshape(N_SPAN, N_CHORD, 4, K).astype(jnp.int32)


def draw_edge_rows(key, part):
    key = jax.random.fold_in(key, 14)
    first, second = jax.random.split(key)
    span_edges = jax.random.randint(first, (N_SPAN - 1, N_CHORD), K // 4, K + 1, jnp.int32)
    span_edges = span_edges.at[0, 0].set(K)
    chord_edges = jax.random.randint(second, (N_SPAN, N_CHORD - 1), K // 4, K + 1, jnp.int32)
    chord_edges = chord_edges.at[0, 0].set(K)
    zero_span = jnp.zeros((1, N_CHORD), jnp.int32)
    zero_chord = jnp.zeros((N_SPAN, 1), jnp.int32)
    lower = jnp.concatenate([zero_span, span_edges], axis=0)
    upper = jnp.concatenate([span_edges, zero_span], axis=0)
    left = jnp.concatenate([zero_chord, chord_edges], axis=1)
    right = jnp.concatenate([chord_edges, zero_chord], axis=1)
    return jnp.stack([lower, upper, left, right], axis=-1)


def draw_corner_rows(key, part):
    key = jax.random.fold_in(key, 15)
    keys = jax.random.split(key, N_SPAN * N_CHORD)
    orders = jax.vmap(lambda single: jax.random.permutation(single, M))(keys)
    return orders[:, :NCORN].reshape(N_SPAN, N_CHORD, NCORN).astype(jnp.int32)


def draw_coarse_inverse(key, part):
    key = jax.random.fold_in(key, 16)
    first, second = jax.random.split(key)
    raw = jnp.clip(jax.random.normal(first, (N_SPAN, CROWS, CROWS), jnp.float32), -4.0, 4.0)
    raw = raw * (0.2 / jnp.sqrt(jnp.float32(CROWS)))
    off = (raw + jnp.swapaxes(raw, 1, 2)) * 0.70710678
    diag = jax.random.uniform(second, (N_SPAN, CROWS), jnp.float32, 0.6, 1.2)
    eye = jnp.eye(CROWS, dtype=jnp.float32)
    return off * (1.0 - eye) + diag[:, :, None] * eye


def touch_ends(array, key, smallest, largest):
    spot = [jax.random.randint(jax.random.fold_in(key, axis), (), 0, length) for axis, length in enumerate(array.shape)]
    main_axis = array.shape.index(max(array.shape))
    next_to = spot[:main_axis] + [(spot[main_axis] + 1) % array.shape[main_axis]] + spot[main_axis + 1:]
    return array.at[tuple(spot)].set(smallest).at[tuple(next_to)].set(largest)


def setup_inputs(seed: int = 0) -> dict:
    splits = jax.random.split(jax.random.key(seed), 8)
    schur = draw_schur(jax.random.fold_in(splits[7], 71), 0)
    loads = draw_loads(jax.random.fold_in(splits[7], 71), 0)
    interface_rows = draw_interface_rows(jax.random.fold_in(splits[7], 71), 0)
    edge_rows = draw_edge_rows(jax.random.fold_in(splits[7], 71), 0)
    corner_rows = draw_corner_rows(jax.random.fold_in(splits[7], 71), 0)
    corner_map = touch_ends(jax.random.randint(splits[5], (N_SPAN, N_CHORD, NCORN), 0, CROWS), jax.random.fold_in(splits[5], 1), 0, CROWS - 1).astype(jnp.int32)
    coarse_inverse = draw_coarse_inverse(jax.random.fold_in(splits[7], 71), 0)
    return {"schur": schur, "loads": loads, "interface_rows": interface_rows, "edge_rows": edge_rows, "corner_rows": corner_rows, "corner_map": corner_map, "coarse_inverse": coarse_inverse}


def place_rows(base, index, values):
    return base.at[:, index].add(values)


def apply_operator(vector, schur, interface_rows, edge_rows):
    span_n, chord_n, cases, unknowns = vector.shape
    width = interface_rows.shape[-1]
    rounded = vector.astype(jnp.bfloat16)
    live = (jnp.arange(width, dtype=jnp.int32)[None, None, None, :] < edge_rows[..., None]).astype(jnp.bfloat16)
    sends = []
    for side in range(4):
        index = jnp.broadcast_to(interface_rows[:, :, side][:, :, None, :], (span_n, chord_n, cases, width))
        sends.append(jnp.take_along_axis(rounded, index, axis=3) * live[:, :, side][:, :, None, :])
    zero_span = jnp.zeros_like(sends[0][:1])
    zero_chord = jnp.zeros_like(sends[0][:, :1])
    from_lower = jnp.concatenate([zero_span, sends[1][:-1]], axis=0)
    from_upper = jnp.concatenate([sends[0][1:], zero_span], axis=0)
    from_left = jnp.concatenate([zero_chord, sends[3][:, :-1]], axis=1)
    from_right = jnp.concatenate([sends[2][:, 1:], zero_chord], axis=1)
    arrived = jnp.concatenate([from_lower, from_upper, from_left, from_right], axis=3).astype(jnp.float32)
    flat_rows = interface_rows.reshape(span_n, chord_n, 4 * width)
    empty = jnp.zeros((span_n, chord_n, cases, unknowns), jnp.float32)
    coupled = jax.vmap(jax.vmap(place_rows))(empty, flat_rows, arrived)

    def local_product(pair):
        field, matrix = pair
        return jnp.einsum("crm,cmn->crn", field.astype(jnp.float32), matrix.astype(jnp.float32),
                          precision=lax.Precision.HIGHEST)

    local = lax.map(local_product, (rounded, schur))
    return local - coupled


def precondition(resid, inv_diag, corner_rows, corner_map, coarse_inverse):
    span_n, chord_n, cases, unknowns = resid.shape
    corners = corner_rows.shape[-1]
    total_rows = coarse_inverse.shape[-1]
    onehot = (corner_map[..., None] == jnp.arange(total_rows, dtype=jnp.int32)).astype(jnp.float32)
    index = jnp.broadcast_to(corner_rows[:, :, None, :], (span_n, chord_n, cases, corners))
    picked = jnp.take_along_axis(resid, index, axis=3)
    coarse = jnp.einsum("scrk,sckm->srm", picked, onehot, precision=lax.Precision.HIGHEST)
    lifted = jnp.einsum("srm,snm->srn", coarse, coarse_inverse, precision=lax.Precision.HIGHEST)
    spread = jnp.broadcast_to(lifted[:, None], (span_n, chord_n, cases, total_rows))
    slot_index = jnp.broadcast_to(corner_map[:, :, None, :], (span_n, chord_n, cases, corners))
    back = jnp.take_along_axis(spread, slot_index, axis=3)
    scaled = resid * inv_diag[:, :, None, :]
    return jax.vmap(jax.vmap(place_rows))(scaled, corner_rows, back)


def case_sum(first, second):
    return jnp.sum(first * second, axis=(0, 1, 3))


def reference(schur, loads, interface_rows, edge_rows, corner_rows, corner_map, coarse_inverse):
    inv_diag = 1.0 / jnp.diagonal(schur, axis1=2, axis2=3).astype(jnp.float32)
    resid = loads.astype(jnp.float32)
    solution = jnp.zeros_like(resid)
    precond = precondition(resid, inv_diag, corner_rows, corner_map, coarse_inverse)
    direction = precond
    norm_now = case_sum(resid, precond)
    for step in range(ITERS):
        image = apply_operator(direction, schur, interface_rows, edge_rows)
        alpha = norm_now / case_sum(direction, image)
        solution = solution + alpha[None, None, :, None] * direction
        resid = resid - alpha[None, None, :, None] * image
        if step + 1 < ITERS:
            precond = precondition(resid, inv_diag, corner_rows, corner_map, coarse_inverse)
            norm_next = case_sum(resid, precond)
            direction = precond + (norm_next / norm_now)[None, None, :, None] * direction
            norm_now = norm_next
    return solution.astype(jnp.bfloat16)
```

```python
import functools

import jax
import jax.numpy as jnp
from jax import lax
from jax.experimental import pallas as pl
from jax.experimental.pallas import tpu as pltpu
from jax.sharding import PartitionSpec as P

ITERS = 5
F32 = jnp.float32
BF16 = jnp.bfloat16
PIVOT_FLOOR = 2e-5
GRAM_ROWS = 16


def with_halo(block, sides, width):
    for axis, dim in sides:
        count = lax.axis_size(axis)
        forward = [(i, i + 1) for i in range(count - 1)]
        backward = [(target, source) for source, target in forward]
        low = lax.ppermute(
            lax.slice_in_dim(block, block.shape[dim] - width, None, axis=dim), axis, forward
        )
        high = lax.ppermute(lax.slice_in_dim(block, 0, width, axis=dim), axis, backward)
        block = jnp.concatenate([low, block, high], axis=dim)
    return block


def case_sum(first, second):
    return lax.psum(jnp.sum(first * second, axis=1), ("span", "chord"))


def plain_recurrence(
    schur, loads, interface_rows, edge_rows, corner_rows, corner_map, coarse_inverse
):
    matrix = schur[0, 0]
    rows = interface_rows[0, 0]
    counts = edge_rows[0, 0]
    corners = corner_rows[0, 0]
    block = coarse_inverse[0]
    width = rows.shape[1]
    unknowns = matrix.shape[0]
    total_rows = block.shape[1]
    live = (jnp.arange(width, dtype=jnp.int32)[None, :] < counts[:, None]).astype(BF16)
    flat_rows = rows.reshape(-1)
    inv_diag = 1.0 / jnp.diagonal(matrix).astype(F32)
    onehot = (
        corner_map[0, 0][:, None] == jnp.arange(total_rows, dtype=jnp.int32)[None, :]
    ).astype(F32)
    highest = lax.Precision.HIGHEST

    def precondition(resid):
        term = jnp.dot(resid[:, corners], onehot, precision=highest)
        summed = lax.psum(term, "chord")
        own_rows = jnp.dot(summed, block.T, precision=highest)
        lifted = lax.all_gather(own_rows, "chord", axis=1, tiled=True)
        back = jnp.dot(lifted, onehot.T, precision=highest)
        return (resid * inv_diag[None, :]).at[:, corners].add(back)

    def apply_operator(direction):
        rounded = direction.astype(BF16)
        picks = [rounded[:, rows[side]] * live[side][None, :] for side in range(4)]
        span_ext = with_halo(jnp.stack([picks[0], picks[1]]), (("span", 0),), 1)
        chord_ext = with_halo(jnp.stack([picks[2], picks[3]]), (("chord", 0),), 1)
        local = jnp.dot(rounded, matrix, preferred_element_type=F32)
        arrived = jnp.concatenate([span_ext[0], span_ext[3], chord_ext[0], chord_ext[3]], axis=1)
        coupled = (
            jnp.zeros((direction.shape[0], unknowns), F32)
            .at[:, flat_rows]
            .add(arrived.astype(F32))
        )
        return local - coupled

    resid = loads[0, 0].astype(F32)
    result = jnp.zeros_like(resid)
    direction = precondition(resid)
    norm_now = case_sum(resid, direction)

    def step(_, carry):
        result, resid, direction, norm_now = carry
        image = apply_operator(direction)
        alpha = norm_now / case_sum(direction, image)
        result = result + alpha[:, None] * direction
        resid = resid - alpha[:, None] * image
        precond = precondition(resid)
        norm_next = case_sum(resid, precond)
        direction = precond + (norm_next / norm_now)[:, None] * direction
        return result, resid, direction, norm_next

    result, resid, direction, norm_now = lax.fori_loop(
        0, ITERS - 1, step, (result, resid, direction, norm_now)
    )
    alpha = norm_now / case_sum(direction, apply_operator(direction))
    return (result + alpha[:, None] * direction).astype(BF16)


NN = (((1,), (0,)), ((), ()))
NT = (((1,), (1,)), ((), ()))
TN = (((0,), (0,)), ((), ()))


def mm(first, second, dims=NN):
    return lax.dot_general(first, second, dims, preferred_element_type=F32)


def halves(value):
    high = value.astype(BF16)
    return high, (value - high.astype(F32)).astype(BF16)


def stacked(value):
    return jnp.concatenate(halves(value), axis=0)


def folded(value):
    half = value.shape[0] // 2
    return value[:half] + value[half:]


def whole(ref, cols=slice(None)):
    half = ref.shape[0] // 2
    return ref[:half, cols].astype(F32) + ref[half:, cols].astype(F32)


def call(body, outs, scratch=(), limit=28, flops=10**8):
    return pl.pallas_call(
        body,
        out_shape=outs,
        scratch_shapes=list(scratch),
        compiler_params=pltpu.CompilerParams(vmem_limit_bytes=limit * 2**20),
        cost_estimate=pl.CostEstimate(flops=flops, bytes_accessed=10**6, transcendentals=0),
    )


def shape(dims, dtype):
    return jax.ShapeDtypeStruct(dims, dtype)


def setup_kernel(
    schur, loads, rows, corners, slots, coarse, pick_ref, corner_ref, inv_ref, send_ref
):
    unknowns = schur.shape[0]
    lanes = corners.shape[1]
    tile = 128
    eye = lax.broadcasted_iota(jnp.int32, (tile, tile), 0) == lax.broadcasted_iota(
        jnp.int32, (tile, tile), 1
    )
    for start in range(0, unknowns, tile):
        block = schur[start : start + tile, start : start + tile].astype(F32)
        diag = jnp.sum(jnp.where(eye, block, 0.0), axis=0, keepdims=True)
        inv_ref[:, start : start + tile] = 1.0 / diag

    def build(step, _):
        start = pl.multiple_of(step * tile, tile)
        index = lax.broadcasted_iota(jnp.int32, (tile, unknowns), 0) + start
        pick_ref[pl.ds(start, tile), :] = (index == rows[...]).astype(F32).astype(BF16)
        index = lax.broadcasted_iota(jnp.int32, (tile, lanes), 0) + start
        corner_ref[pl.ds(start, tile), :] = (index == corners[...]).astype(F32).astype(BF16)
        return 0

    lax.fori_loop(0, unknowns // tile, build, 0)
    picked = mm(loads[...], corner_ref[...])
    cases = picked.shape[0]
    own, total = coarse.shape
    for peer in range(send_ref.shape[0]):
        send_ref[peer, :cases, :] = picked
        for part in range(total // lanes):
            send_ref[peer, cases + part * own : cases + (part + 1) * own, :] = coarse[
                :, part * lanes : (part + 1) * lanes
            ]
        send_ref[peer, cases + own * (total // lanes) :, :] = jnp.broadcast_to(
            slots[...].astype(F32), (8, lanes)
        )


def lift_kernel(slots, got, lift_ref, *, cases, own):
    peers, _, lanes = got.shape
    total = own * peers
    parts = total // lanes
    index = lax.broadcasted_iota(jnp.int32, (total, lanes), 0)
    mine = (index == slots[...]).astype(F32).astype(BF16)
    inverse = jnp.concatenate(
        [
            jnp.concatenate(
                [got[p, cases + q * own : cases + (q + 1) * own, :] for q in range(parts)], axis=1
            )
            for p in range(peers)
        ],
        axis=0,
    )
    high = inverse.astype(BF16)
    rest = inverse - high.astype(F32)
    middle, low = halves(rest)
    cols = (mm(high, mine) + mm(middle, mine)) + mm(low, mine)
    cols = jnp.concatenate(halves(cols), axis=1)
    base = cases + own * parts
    for peer in range(peers):
        theirs = got[peer, base : base + 1, :].astype(jnp.int32)
        theirs = (index == theirs).astype(F32).astype(BF16)
        lift_ref[peer * lanes : (peer + 1) * lanes, :] = mm(theirs, cols, TN).astype(BF16)


def precondition_kernel(got, lift, corner, pick, resid, inv, field_ref, *send_refs):
    peers = got.shape[0]
    cases = resid.shape[0]
    lanes = corner.shape[1]
    corners = jnp.concatenate([got[p, :cases, :] for p in range(peers)], axis=1)
    product = mm(stacked(corners), lift[...])
    back = folded(product[:, :lanes]) + product[:cases, lanes:]
    back = stacked(back)
    unknowns = resid.shape[1]
    width = unknowns // 4
    for side in range(4):
        cols = slice(side * width, (side + 1) * width)
        added = folded(mm(back, corner[cols, :], NT))
        value = resid[:, cols].astype(F32) * inv[:, cols] + added
        high, low = halves(value)
        field_ref[:cases, cols] = high
        field_ref[cases:, cols] = low
    for pair in range(2):
        cols = slice(2 * pair * width, 2 * (pair + 1) * width)
        sent = mm(field_ref[...], pick[:, cols]).astype(BF16)
        send_refs[2 * pair][...] = sent[:, :width]
        send_refs[2 * pair + 1][...] = sent[:, width:]


def gram_slot(row, col):
    return col * (col + 1) // 2 + row + 5 if row >= 0 else col


def local_kernel(*refs, step):
    field, matrix, loads, acc = refs[:4]
    last = step == ITERS - 1
    before = refs[4] if step else None
    images = refs[5 : 5 + step] if step else ()
    out_acc = refs[-1]
    cases = loads.shape[0]
    lane = lax.broadcasted_iota(jnp.int32, (cases, 128), 1)
    total = acc[...] if step else jnp.zeros((cases, 128), F32)

    def put(total, slot, value):
        return jnp.where(lane == slot, value, total)

    def product(first, second):
        return jnp.sum(first * second, axis=1, keepdims=True)

    local = folded(mm(field[...], matrix[...]))
    value = whole(field)
    if last:
        total = put(total, gram_slot(step, step), product(value, local))
    else:
        refs[-2][...] = local
    total = put(total, gram_slot(-1, step), product(value, loads[...].astype(F32)))
    for row in range(step):
        total = put(total, gram_slot(row, step), product(value, images[row][...]))
    if step:
        total = put(total, gram_slot(step - 1, step - 1), product(whole(before), images[-1][...]))
    out_acc[...] = total


def image_kernel(from0, from1, from2, from3, pick, corner, local, image_ref, send_ref, joined):
    width = from0.shape[1]
    for side, came in enumerate((from0, from1, from2, from3)):
        joined[:, side * width : (side + 1) * width] = came[...]
    unknowns = local.shape[1]
    chunk = 512
    for start in range(0, unknowns, chunk):
        cols = slice(start, start + chunk)
        image_ref[:, cols] = local[:, cols] - folded(mm(joined[...], pick[cols, :], NT))
    picked = folded(mm(stacked(image_ref[...]), corner[...]))
    for peer in range(send_ref.shape[0]):
        send_ref[peer] = picked


def gram_kernel(acc, sent0, from0, sent2, from2, send_ref):
    total = acc[...]
    lane = lax.broadcasted_iota(jnp.int32, total.shape, 1)
    pairs = whole(sent0) * whole(from0) + whole(sent2) * whole(from2)
    coupled = 2.0 * jnp.sum(pairs, axis=1, keepdims=True)
    slot = gram_slot(ITERS - 1, ITERS - 1)
    total = jnp.where(lane == slot, total - coupled, total).T
    packed = jnp.concatenate([total[:GRAM_ROWS], total[GRAM_ROWS : 2 * GRAM_ROWS]], axis=1)
    for peer in range(send_ref.shape[0]):
        send_ref[peer] = packed


def tree_sum(parts):
    while len(parts) > 1:
        parts = [a + b for a, b in zip(parts[::2], parts[1::2])] + parts[len(parts) & ~1 :]
    return parts[0]


def relay_kernel(got, send_ref):
    total = tree_sum([got[p] for p in range(got.shape[0])])
    for peer in range(send_ref.shape[0]):
        send_ref[peer] = total


def solve_kernel(got, *refs):
    fields = refs[:ITERS]
    out_ref, fault_ref = refs[ITERS:]
    total = tree_sum([got[p] for p in range(got.shape[0])])
    cases = out_ref.shape[0]

    def entry(row, col):
        slot = gram_slot(row, col)
        half, at = divmod(slot, GRAM_ROWS)
        return total[at : at + 1, half * cases : (half + 1) * cases]

    n = ITERS
    scale = [lax.rsqrt(entry(k, k)) for k in range(n)]
    rhs = [entry(-1, k) * scale[k] for k in range(n)]
    lower, pivots, solved = {}, [], []
    fault = jnp.zeros_like(rhs[0])
    for k in range(n):
        for j in range(k):
            value = (entry(j, k) * scale[j]) * scale[k]
            for m in range(j):
                value = value - (lower[k, m] * pivots[m]) * lower[j, m]
            lower[k, j] = value / pivots[j]
        pivot = jnp.ones_like(rhs[0])
        value = rhs[k]
        for m in range(k):
            pivot = pivot - (lower[k, m] * pivots[m]) * lower[k, m]
            value = value - lower[k, m] * solved[m]
        pivots.append(pivot)
        solved.append(value)
        good = (pivot > PIVOT_FLOOR) & (scale[k] > 0.0) & (scale[k] < 1e30)
        fault = jnp.maximum(fault, jnp.where(good, 0.0, 1.0))
    coeffs = [solved[k] / pivots[k] for k in range(n)]
    for k in reversed(range(n)):
        for m in range(k + 1, n):
            coeffs[k] = coeffs[k] - lower[m, k] * coeffs[m]
    coeffs = [coeffs[k] * scale[k] for k in range(n)]
    for k in range(n):
        good = jnp.abs(coeffs[k]) < 1e37
        fault = jnp.maximum(fault, jnp.where(good, 0.0, 1.0))
    fault_ref[0, 0] = jnp.max(fault)
    spread = jnp.concatenate(coeffs + [jnp.zeros_like(coeffs[0])] * (8 - n), axis=0)
    spread = jnp.concatenate([spread, jnp.zeros_like(spread)], axis=1).T[:cases]
    width = out_ref.shape[1] // 4
    for part in range(4):
        cols = slice(part * width, (part + 1) * width)
        value = spread[:, 0:1] * whole(fields[0], cols)
        for k in range(1, n):
            value = value + spread[:, k : k + 1] * whole(fields[k], cols)
        out_ref[:, cols] = value.astype(BF16)


def ring(axis, shift):
    count = lax.axis_size(axis)
    return [(i, (i + shift) % count) for i in range(count)]


def exchange(send, axis, groups=None):
    return lax.all_to_all(send, axis, 0, 0, axis_index_groups=groups)


def sum_groups(span, chord, inner):
    outer = span // inner
    first = [
        [(o * inner + i) * chord + c for o in range(outer) for c in range(chord)]
        for i in range(inner)
    ]
    second = [[o * inner + i for i in range(inner)] for o in range(outer)]
    return first, second


def shards(schur, loads, interface_rows, edge_rows, corner_rows, corner_map, coarse_inverse):
    originals = (
        schur, loads, interface_rows, edge_rows, corner_rows, corner_map, coarse_inverse
    )
    span, chord = lax.axis_size("span"), lax.axis_size("chord")
    matrix, rhs, block = schur[0, 0], loads[0, 0], coarse_inverse[0]
    unknowns = matrix.shape[0]
    cases = rhs.shape[0]
    rows, counts = interface_rows[0, 0], edge_rows[0, 0]
    width = rows.shape[1]
    lanes = corner_rows.shape[2]
    own, total = block.shape
    live = jnp.arange(width, dtype=jnp.int32)[None, :] < counts[:, None]
    live_rows = jnp.where(live, rows, -1).reshape(1, unknowns)
    slots = corner_map[0]

    pick, corner, inv, send = call(
        setup_kernel,
        (
            shape((unknowns, unknowns), BF16),
            shape((unknowns, lanes), BF16),
            shape((1, unknowns), F32),
            shape((chord, cases + own * (total // lanes) + 8, lanes), F32),
        ),
    )(matrix, rhs, live_rows, corner_rows[0], slots, block)
    got = exchange(send, "chord")
    lift = call(
        functools.partial(lift_kernel, cases=cases, own=own),
        shape((chord * lanes, 2 * lanes), BF16),
    )(slots, got)

    resid = rhs
    fields, images = [], []
    acc = jnp.zeros((cases, 128), F32)
    for step in range(ITERS):
        field, *sends = call(
            precondition_kernel,
            (shape((2 * cases, unknowns), BF16),) + (shape((2 * cases, width), BF16),) * 4,
        )(got, lift, corner, pick, resid, inv)
        last = step == ITERS - 1
        came = [
            lax.ppermute(sends[1], "span", ring("span", 1)),
            None if last else lax.ppermute(sends[0], "span", ring("span", -1)),
            lax.ppermute(sends[3], "chord", ring("chord", 1)),
            None if last else lax.ppermute(sends[2], "chord", ring("chord", -1)),
        ]
        out = (shape((cases, 128), F32),)
        if not last:
            out = (shape((cases, unknowns), F32),) + out
        before = (fields[-1],) if step else ()
        result = call(functools.partial(local_kernel, step=step), out)(
            field, matrix, rhs, acc, *before, *images
        )
        acc = result[-1]
        fields.append(field)
        if not last:
            resid, send = call(
                image_kernel,
                (shape((cases, unknowns), F32), shape((chord, cases, lanes), F32)),
                scratch=[pltpu.VMEM((2 * cases, unknowns), BF16)],
            )(*came, pick, corner, result[0])
            images.append(resid)
            got = exchange(send, "chord")

    inner = 16 if span % 16 == 0 else span
    first, second = sum_groups(span, chord, inner)
    send = call(gram_kernel, shape((len(first[0]), GRAM_ROWS, 128), F32))(
        acc, sends[0], came[0], sends[2], came[2]
    )
    got = exchange(send, ("span", "chord"), first)
    send = call(relay_kernel, shape((inner, GRAM_ROWS, 128), F32))(got)
    got = exchange(send, "span", second)
    answer, fault = pl.pallas_call(
        solve_kernel,
        out_shape=(shape((cases, unknowns), BF16), shape((1, 1), F32)),
        out_specs=(
            pl.BlockSpec(memory_space=pltpu.VMEM),
            pl.BlockSpec(memory_space=pltpu.SMEM),
        ),
        compiler_params=pltpu.CompilerParams(vmem_limit_bytes=28 * 2**20),
    )(got, *fields)
    answer = lax.cond(
        fault[0, 0] > 0.0,
        lambda answer, *arrays: plain_recurrence(*arrays),
        lambda answer, *arrays: answer,
        answer,
        *originals,
    )
    return answer[None, None]


def solution(mesh):
    return jax.shard_map(
        shards,
        mesh=mesh,
        in_specs=(
            P("span", "chord", None, None),
            P("span", "chord", None, None),
            P("span", "chord", None, None),
            P("span", "chord", None),
            P("span", "chord", None),
            P("span", "chord", None),
            P("span", "chord", None),
        ),
        out_specs=P("span", "chord", None, None),
        check_vma=False,
    )
```

```python
import functools

import jax
import jax.numpy as jnp
from jax import lax
from jax.experimental import pallas as pl
from jax.experimental.pallas import tpu as pltpu
from jax.sharding import PartitionSpec as P

ITERS = 5
F32 = jnp.float32
BF16 = jnp.bfloat16
PIVOT_FLOOR = 2e-5
GRAM_ROWS = 16


def with_halo(block, sides, width):
    for axis, dim in sides:
        count = lax.axis_size(axis)
        forward = [(i, i + 1) for i in range(count - 1)]
        backward = [(target, source) for source, target in forward]
        low = lax.ppermute(
            lax.slice_in_dim(block, block.shape[dim] - width, None, axis=dim), axis, forward
        )
        high = lax.ppermute(lax.slice_in_dim(block, 0, width, axis=dim), axis, backward)
        block = jnp.concatenate([low, block, high], axis=dim)
    return block


def case_sum(first, second):
    return lax.psum(jnp.sum(first * second, axis=1), ("span", "chord"))


def plain_recurrence(
    schur, loads, interface_rows, edge_rows, corner_rows, corner_map, coarse_inverse
):
    matrix = schur[0, 0]
    rows = interface_rows[0, 0]
    counts = edge_rows[0, 0]
    corners = corner_rows[0, 0]
    block = coarse_inverse[0]
    width = rows.shape[1]
    unknowns = matrix.shape[0]
    total_rows = block.shape[1]
    live = (jnp.arange(width, dtype=jnp.int32)[None, :] < counts[:, None]).astype(BF16)
    flat_rows = rows.reshape(-1)
    inv_diag = 1.0 / jnp.diagonal(matrix).astype(F32)
    onehot = (
        corner_map[0, 0][:, None] == jnp.arange(total_rows, dtype=jnp.int32)[None, :]
    ).astype(F32)
    highest = lax.Precision.HIGHEST

    def precondition(resid):
        term = jnp.dot(resid[:, corners], onehot, precision=highest)
        summed = lax.psum(term, "chord")
        own_rows = jnp.dot(summed, block.T, precision=highest)
        lifted = lax.all_gather(own_rows, "chord", axis=1, tiled=True)
        back = jnp.dot(lifted, onehot.T, precision=highest)
        return (resid * inv_diag[None, :]).at[:, corners].add(back)

    def apply_operator(direction):
        rounded = direction.astype(BF16)
        picks = [rounded[:, rows[side]] * live[side][None, :] for side in range(4)]
        span_ext = with_halo(jnp.stack([picks[0], picks[1]]), (("span", 0),), 1)
        chord_ext = with_halo(jnp.stack([picks[2], picks[3]]), (("chord", 0),), 1)
        local = jnp.dot(rounded, matrix, preferred_element_type=F32)
        arrived = jnp.concatenate([span_ext[0], span_ext[3], chord_ext[0], chord_ext[3]], axis=1)
        coupled = (
            jnp.zeros((direction.shape[0], unknowns), F32)
            .at[:, flat_rows]
            .add(arrived.astype(F32))
        )
        return local - coupled

    resid = loads[0, 0].astype(F32)
    result = jnp.zeros_like(resid)
    direction = precondition(resid)
    norm_now = case_sum(resid, direction)

    def step(_, carry):
        result, resid, direction, norm_now = carry
        image = apply_operator(direction)
        alpha = norm_now / case_sum(direction, image)
        result = result + alpha[:, None] * direction
        resid = resid - alpha[:, None] * image
        precond = precondition(resid)
        norm_next = case_sum(resid, precond)
        direction = precond + (norm_next / norm_now)[:, None] * direction
        return result, resid, direction, norm_next

    result, resid, direction, norm_now = lax.fori_loop(
        0, ITERS - 1, step, (result, resid, direction, norm_now)
    )
    alpha = norm_now / case_sum(direction, apply_operator(direction))
    return (result + alpha[:, None] * direction).astype(BF16)


NN = (((1,), (0,)), ((), ()))
NT = (((1,), (1,)), ((), ()))
TN = (((0,), (0,)), ((), ()))


def mm(first, second, dims=NN):
    return lax.dot_general(first, second, dims, preferred_element_type=F32)


def halves(value):
    high = value.astype(BF16)
    return high, (value - high.astype(F32)).astype(BF16)


def stacked(value):
    return jnp.concatenate(halves(value), axis=0)


def folded(value):
    half = value.shape[0] // 2
    return value[:half] + value[half:]


def whole(ref, cols=slice(None)):
    half = ref.shape[0] // 2
    return ref[:half, cols].astype(F32) + ref[half:, cols].astype(F32)


def call(body, outs, scratch=(), limit=28, flops=10**8):
    return pl.pallas_call(
        body,
        out_shape=outs,
        scratch_shapes=list(scratch),
        compiler_params=pltpu.CompilerParams(vmem_limit_bytes=limit * 2**20),
        cost_estimate=pl.CostEstimate(flops=flops, bytes_accessed=10**6, transcendentals=0),
    )


def shape(dims, dtype):
    return jax.ShapeDtypeStruct(dims, dtype)


def setup_kernel(
    counts, loads, rows, corners, slots, coarse, pick_ref, corner_ref, send_ref
):
    unknowns = loads.shape[1]
    lanes = corners.shape[1]
    tile = 128

    sides, width = rows.shape
    lane = lax.broadcasted_iota(jnp.int32, (1, width), 1)
    live = [jnp.where(lane < counts[side], rows[side : side + 1, :], -1) for side in range(sides)]

    def build(step, _):
        start = pl.multiple_of(step * tile, tile)
        index = lax.broadcasted_iota(jnp.int32, (tile, width), 0) + start
        for side in range(sides):
            cols = slice(side * width, (side + 1) * width)
            pick_ref[pl.ds(start, tile), cols] = (index == live[side]).astype(F32).astype(BF16)
        index = lax.broadcasted_iota(jnp.int32, (tile, lanes), 0) + start
        corner_ref[pl.ds(start, tile), :] = (index == corners[...]).astype(F32).astype(BF16)
        return 0

    lax.fori_loop(0, unknowns // tile, build, 0)
    picked = mm(loads[...], corner_ref[...])
    cases = picked.shape[0]
    own, total = coarse.shape
    for peer in range(send_ref.shape[0]):
        send_ref[peer, :cases, :] = picked
        for part in range(total // lanes):
            send_ref[peer, cases + part * own : cases + (part + 1) * own, :] = coarse[
                :, part * lanes : (part + 1) * lanes
            ]
        send_ref[peer, cases + own * (total // lanes) :, :] = jnp.broadcast_to(
            slots[...].astype(F32), (8, lanes)
        )


def lift_kernel(schur, slots, got, lift_ref, inv_ref, *, cases, own):
    tile = 128
    eye = lax.broadcasted_iota(jnp.int32, (tile, tile), 0) == lax.broadcasted_iota(
        jnp.int32, (tile, tile), 1
    )
    for start in range(0, schur.shape[0], tile):
        block = schur[start : start + tile, start : start + tile].astype(F32)
        diag = jnp.sum(jnp.where(eye, block, 0.0), axis=0, keepdims=True)
        inv_ref[:, start : start + tile] = 1.0 / diag
    peers, _, lanes = got.shape
    total = own * peers
    parts = total // lanes
    index = lax.broadcasted_iota(jnp.int32, (total, lanes), 0)
    mine = (index == slots[...]).astype(F32).astype(BF16)
    inverse = jnp.concatenate(
        [
            jnp.concatenate(
                [got[p, cases + q * own : cases + (q + 1) * own, :] for q in range(parts)], axis=1
            )
            for p in range(peers)
        ],
        axis=0,
    )
    high = inverse.astype(BF16)
    rest = inverse - high.astype(F32)
    middle, low = halves(rest)
    cols = (mm(high, mine) + mm(middle, mine)) + mm(low, mine)
    cols = jnp.concatenate(halves(cols), axis=1)
    base = cases + own * parts
    for peer in range(peers):
        theirs = got[peer, base : base + 1, :].astype(jnp.int32)
        theirs = (index == theirs).astype(F32).astype(BF16)
        lift_ref[peer * lanes : (peer + 1) * lanes, :] = mm(theirs, cols, TN).astype(BF16)


def precondition_kernel(got, lift, corner, pick, resid, inv, field_ref, *send_refs):
    peers = got.shape[0]
    cases = resid.shape[0]
    lanes = corner.shape[1]
    corners = jnp.concatenate([got[p, :cases, :] for p in range(peers)], axis=1)
    product = mm(stacked(corners), lift[...])
    back = folded(product[:, :lanes]) + product[:cases, lanes:]
    back = stacked(back)
    unknowns = resid.shape[1]
    width = unknowns // 4
    for side in range(4):
        cols = slice(side * width, (side + 1) * width)
        added = folded(mm(back, corner[cols, :], NT))
        value = resid[:, cols].astype(F32) * inv[:, cols] + added
        high, low = halves(value)
        field_ref[:cases, cols] = high
        field_ref[cases:, cols] = low
    for pair in range(2):
        cols = slice(2 * pair * width, 2 * (pair + 1) * width)
        sent = mm(field_ref[...], pick[:, cols]).astype(BF16)
        send_refs[2 * pair][...] = sent[:, :width]
        send_refs[2 * pair + 1][...] = sent[:, width:]


def gram_slot(row, col):
    return col * (col + 1) // 2 + row + 5 if row >= 0 else col


def local_kernel(*refs, step):
    field, matrix, loads, acc = refs[:4]
    last = step == ITERS - 1
    before = refs[4] if step else None
    images = refs[5 : 5 + step] if step else ()
    out_acc = refs[-1]
    cases = loads.shape[0]
    lane = lax.broadcasted_iota(jnp.int32, (cases, 128), 1)
    total = acc[...] if step else jnp.zeros((cases, 128), F32)

    def put(total, slot, value):
        return jnp.where(lane == slot, value, total)

    def product(first, second):
        return jnp.sum(first * second, axis=1, keepdims=True)

    local = folded(mm(field[...], matrix[...]))
    value = whole(field)
    if last:
        total = put(total, gram_slot(step, step), product(value, local))
    else:
        refs[-2][...] = local
    total = put(total, gram_slot(-1, step), product(value, loads[...].astype(F32)))
    for row in range(step):
        total = put(total, gram_slot(row, step), product(value, images[row][...]))
    if step:
        total = put(total, gram_slot(step - 1, step - 1), product(whole(before), images[-1][...]))
    out_acc[...] = total


def image_kernel(from0, from1, from2, from3, pick, corner, local, image_ref, send_ref, joined):
    width = from0.shape[1]
    for side, came in enumerate((from0, from1, from2, from3)):
        joined[:, side * width : (side + 1) * width] = came[...]
    unknowns = local.shape[1]
    chunk = 512
    for start in range(0, unknowns, chunk):
        cols = slice(start, start + chunk)
        image_ref[:, cols] = local[:, cols] - folded(mm(joined[...], pick[cols, :], NT))
    picked = folded(mm(stacked(image_ref[...]), corner[...]))
    for peer in range(send_ref.shape[0]):
        send_ref[peer] = picked


def gram_kernel(acc, sent0, from0, sent2, from2, send_ref):
    total = acc[...]
    lane = lax.broadcasted_iota(jnp.int32, total.shape, 1)
    pairs = whole(sent0) * whole(from0) + whole(sent2) * whole(from2)
    coupled = 2.0 * jnp.sum(pairs, axis=1, keepdims=True)
    slot = gram_slot(ITERS - 1, ITERS - 1)
    total = jnp.where(lane == slot, total - coupled, total).T
    packed = jnp.concatenate([total[:GRAM_ROWS], total[GRAM_ROWS : 2 * GRAM_ROWS]], axis=1)
    for peer in range(send_ref.shape[0]):
        send_ref[peer] = packed


def tree_sum(parts):
    while len(parts) > 1:
        parts = [a + b for a, b in zip(parts[::2], parts[1::2])] + parts[len(parts) & ~1 :]
    return parts[0]


def relay_kernel(got, send_ref):
    total = tree_sum([got[p] for p in range(got.shape[0])])
    for peer in range(send_ref.shape[0]):
        send_ref[peer] = total


def solve_kernel(got, *refs):
    fields = refs[:ITERS]
    out_ref, fault_ref = refs[ITERS:]
    total = tree_sum([got[p] for p in range(got.shape[0])])
    cases = out_ref.shape[0]

    def entry(row, col):
        slot = gram_slot(row, col)
        half, at = divmod(slot, GRAM_ROWS)
        return total[at : at + 1, half * cases : (half + 1) * cases]

    n = ITERS
    scale = [lax.rsqrt(entry(k, k)) for k in range(n)]
    rhs = [entry(-1, k) * scale[k] for k in range(n)]
    lower, pivots, solved = {}, [], []
    fault = jnp.zeros_like(rhs[0])
    for k in range(n):
        for j in range(k):
            value = (entry(j, k) * scale[j]) * scale[k]
            for m in range(j):
                value = value - (lower[k, m] * pivots[m]) * lower[j, m]
            lower[k, j] = value / pivots[j]
        pivot = jnp.ones_like(rhs[0])
        value = rhs[k]
        for m in range(k):
            pivot = pivot - (lower[k, m] * pivots[m]) * lower[k, m]
            value = value - lower[k, m] * solved[m]
        pivots.append(pivot)
        solved.append(value)
        good = (pivot > PIVOT_FLOOR) & (scale[k] > 0.0) & (scale[k] < 1e30)
        fault = jnp.maximum(fault, jnp.where(good, 0.0, 1.0))
    coeffs = [solved[k] / pivots[k] for k in range(n)]
    for k in reversed(range(n)):
        for m in range(k + 1, n):
            coeffs[k] = coeffs[k] - lower[m, k] * coeffs[m]
    coeffs = [coeffs[k] * scale[k] for k in range(n)]
    for k in range(n):
        good = jnp.abs(coeffs[k]) < 1e37
        fault = jnp.maximum(fault, jnp.where(good, 0.0, 1.0))
    fault_ref[0, 0] = jnp.max(fault)
    spread = jnp.concatenate(coeffs + [jnp.zeros_like(coeffs[0])] * (8 - n), axis=0)
    spread = jnp.concatenate([spread, jnp.zeros_like(spread)], axis=1).T[:cases]
    width = out_ref.shape[1] // 4
    for part in range(4):
        cols = slice(part * width, (part + 1) * width)
        value = spread[:, 0:1] * whole(fields[0], cols)
        for k in range(1, n):
            value = value + spread[:, k : k + 1] * whole(fields[k], cols)
        out_ref[:, cols] = value.astype(BF16)


def shifted(value, axis, shift, wrap):
    count = lax.axis_size(axis)
    pairs = [(i, (i + shift) % count) for i in range(count) if wrap or 0 <= i + shift < count]
    return lax.ppermute(value, axis, pairs)


def exchange(send, axis, groups=None):
    return lax.all_to_all(send, axis, 0, 0, axis_index_groups=groups)


def sum_groups(span, chord, inner):
    outer = span // inner
    first = [
        [(o * inner + i) * chord + c for o in range(outer) for c in range(chord)]
        for i in range(inner)
    ]
    second = [[o * inner + i for i in range(inner)] for o in range(outer)]
    return first, second


def shards(schur, loads, interface_rows, edge_rows, corner_rows, corner_map, coarse_inverse):
    originals = (
        schur, loads, interface_rows, edge_rows, corner_rows, corner_map, coarse_inverse
    )
    span, chord = lax.axis_size("span"), lax.axis_size("chord")
    matrix, rhs, block = schur[0, 0], loads[0, 0], coarse_inverse[0]
    unknowns = matrix.shape[0]
    cases = rhs.shape[0]
    rows, counts = interface_rows[0, 0], edge_rows[0, 0]
    width = rows.shape[1]
    lanes = corner_rows.shape[2]
    own, total = block.shape
    slots = corner_map[0]

    pick, corner, send = pl.pallas_call(
        setup_kernel,
        in_specs=[pl.BlockSpec(memory_space=pltpu.SMEM)]
        + [pl.BlockSpec(memory_space=pltpu.VMEM)] * 5,
        out_shape=(
            shape((unknowns, unknowns), BF16),
            shape((unknowns, lanes), BF16),
            shape((chord, cases + own * (total // lanes) + 8, lanes), F32),
        ),
        compiler_params=pltpu.CompilerParams(vmem_limit_bytes=28 * 2**20),
    )(counts, rhs, rows, corner_rows[0], slots, block)
    got = exchange(send, "chord")
    lift, inv = call(
        functools.partial(lift_kernel, cases=cases, own=own),
        (shape((chord * lanes, 2 * lanes), BF16), shape((1, unknowns), F32)),
    )(matrix, slots, got)

    resid = rhs
    fields, images = [], []
    acc = jnp.zeros((cases, 128), F32)
    for step in range(ITERS):
        field, *sends = call(
            precondition_kernel,
            (shape((2 * cases, unknowns), BF16),) + (shape((2 * cases, width), BF16),) * 4,
        )(got, lift, corner, pick, resid, inv)
        last = step == ITERS - 1
        came = [
            shifted(sends[1], "span", 1, False),
            None if last else shifted(sends[0], "span", -1, False),
            shifted(sends[3], "chord", 1, True),
            None if last else shifted(sends[2], "chord", -1, True),
        ]
        out = (shape((cases, 128), F32),)
        if not last:
            out = (shape((cases, unknowns), F32),) + out
        before = (fields[-1],) if step else ()
        result = call(functools.partial(local_kernel, step=step), out)(
            field, matrix, rhs, acc, *before, *images
        )
        acc = result[-1]
        fields.append(field)
        if not last:
            resid, send = call(
                image_kernel,
                (shape((cases, unknowns), F32), shape((chord, cases, lanes), F32)),
                scratch=[pltpu.VMEM((2 * cases, unknowns), BF16)],
            )(*came, pick, corner, result[0])
            images.append(resid)
            got = exchange(send, "chord")

    inner = 16 if span % 16 == 0 else span
    first, second = sum_groups(span, chord, inner)
    send = call(gram_kernel, shape((len(first[0]), GRAM_ROWS, 128), F32))(
        acc, sends[0], came[0], sends[2], came[2]
    )
    got = exchange(send, ("span", "chord"), first)
    send = call(relay_kernel, shape((inner, GRAM_ROWS, 128), F32))(got)
    got = exchange(send, "span", second)
    answer, fault = pl.pallas_call(
        solve_kernel,
        out_shape=(shape((cases, unknowns), BF16), shape((1, 1), F32)),
        out_specs=(
            pl.BlockSpec(memory_space=pltpu.VMEM),
            pl.BlockSpec(memory_space=pltpu.SMEM),
        ),
        compiler_params=pltpu.CompilerParams(vmem_limit_bytes=28 * 2**20),
    )(got, *fields)
    answer = lax.cond(
        fault[0, 0] > 0.0,
        lambda answer, *arrays: plain_recurrence(*arrays),
        lambda answer, *arrays: answer,
        answer,
        *originals,
    )
    return answer[None, None]


def solution(mesh):
    return jax.shard_map(
        shards,
        mesh=mesh,
        in_specs=(
            P("span", "chord", None, None),
            P("span", "chord", None, None),
            P("span", "chord", None, None),
            P("span", "chord", None),
            P("span", "chord", None),
            P("span", "chord", None),
            P("span", "chord", None),
        ),
        out_specs=P("span", "chord", None, None),
        check_vma=False,
    )
```

```python
import functools

import jax
import jax.numpy as jnp
from jax import lax
from jax.experimental import pallas as pl
from jax.experimental.pallas import tpu as pltpu
from jax.sharding import PartitionSpec as P

ITERS = 5
F32 = jnp.float32
BF16 = jnp.bfloat16
PIVOT_FLOOR = 2e-5
GRAM_ROWS = 16


def with_halo(block, sides, width):
    for axis, dim in sides:
        count = lax.axis_size(axis)
        forward = [(i, i + 1) for i in range(count - 1)]
        backward = [(target, source) for source, target in forward]
        low = lax.ppermute(
            lax.slice_in_dim(block, block.shape[dim] - width, None, axis=dim), axis, forward
        )
        high = lax.ppermute(lax.slice_in_dim(block, 0, width, axis=dim), axis, backward)
        block = jnp.concatenate([low, block, high], axis=dim)
    return block


def case_sum(first, second):
    return lax.psum(jnp.sum(first * second, axis=1), ("span", "chord"))


def plain_recurrence(
    schur, loads, interface_rows, edge_rows, corner_rows, corner_map, coarse_inverse
):
    matrix = schur[0, 0]
    rows = interface_rows[0, 0]
    counts = edge_rows[0, 0]
    corners = corner_rows[0, 0]
    block = coarse_inverse[0]
    width = rows.shape[1]
    unknowns = matrix.shape[0]
    total_rows = block.shape[1]
    live = (jnp.arange(width, dtype=jnp.int32)[None, :] < counts[:, None]).astype(BF16)
    flat_rows = rows.reshape(-1)
    inv_diag = 1.0 / jnp.diagonal(matrix).astype(F32)
    onehot = (
        corner_map[0, 0][:, None] == jnp.arange(total_rows, dtype=jnp.int32)[None, :]
    ).astype(F32)
    highest = lax.Precision.HIGHEST

    def precondition(resid):
        term = jnp.dot(resid[:, corners], onehot, precision=highest)
        summed = lax.psum(term, "chord")
        own_rows = jnp.dot(summed, block.T, precision=highest)
        lifted = lax.all_gather(own_rows, "chord", axis=1, tiled=True)
        back = jnp.dot(lifted, onehot.T, precision=highest)
        return (resid * inv_diag[None, :]).at[:, corners].add(back)

    def apply_operator(direction):
        rounded = direction.astype(BF16)
        picks = [rounded[:, rows[side]] * live[side][None, :] for side in range(4)]
        span_ext = with_halo(jnp.stack([picks[0], picks[1]]), (("span", 0),), 1)
        chord_ext = with_halo(jnp.stack([picks[2], picks[3]]), (("chord", 0),), 1)
        local = jnp.dot(rounded, matrix, preferred_element_type=F32)
        arrived = jnp.concatenate([span_ext[0], span_ext[3], chord_ext[0], chord_ext[3]], axis=1)
        coupled = (
            jnp.zeros((direction.shape[0], unknowns), F32)
            .at[:, flat_rows]
            .add(arrived.astype(F32))
        )
        return local - coupled

    resid = loads[0, 0].astype(F32)
    result = jnp.zeros_like(resid)
    direction = precondition(resid)
    norm_now = case_sum(resid, direction)

    def step(_, carry):
        result, resid, direction, norm_now = carry
        image = apply_operator(direction)
        alpha = norm_now / case_sum(direction, image)
        result = result + alpha[:, None] * direction
        resid = resid - alpha[:, None] * image
        precond = precondition(resid)
        norm_next = case_sum(resid, precond)
        direction = precond + (norm_next / norm_now)[:, None] * direction
        return result, resid, direction, norm_next

    result, resid, direction, norm_now = lax.fori_loop(
        0, ITERS - 1, step, (result, resid, direction, norm_now)
    )
    alpha = norm_now / case_sum(direction, apply_operator(direction))
    return (result + alpha[:, None] * direction).astype(BF16)


NN = (((1,), (0,)), ((), ()))
NT = (((1,), (1,)), ((), ()))
TN = (((0,), (0,)), ((), ()))


def mm(first, second, dims=NN):
    return lax.dot_general(first, second, dims, preferred_element_type=F32)


def halves(value):
    high = value.astype(BF16)
    return high, (value - high.astype(F32)).astype(BF16)


def stacked(value):
    return jnp.concatenate(halves(value), axis=0)


def folded(value):
    half = value.shape[0] // 2
    return value[:half] + value[half:]


def call(body, outs, scratch=(), limit=28, flops=10**8):
    return pl.pallas_call(
        body,
        out_shape=outs,
        scratch_shapes=list(scratch),
        compiler_params=pltpu.CompilerParams(vmem_limit_bytes=limit * 2**20),
        cost_estimate=pl.CostEstimate(flops=flops, bytes_accessed=10**6, transcendentals=0),
    )


def shape(dims, dtype):
    return jax.ShapeDtypeStruct(dims, dtype)


def setup_kernel(
    counts, schur, loads, rows, corners, slots, coarse,
    pick_ref, corner_ref, inv_ref, send_ref, blocks, sems,
):
    unknowns = loads.shape[1]
    lanes = corners.shape[1]
    tile = blocks.shape[1]
    copies = []
    for part in range(unknowns // tile):
        span = pl.ds(part * tile, tile)
        copy = pltpu.make_async_copy(schur.at[span, span], blocks.at[part], sems.at[part])
        copy.start()
        copies.append(copy)

    sides, width = rows.shape
    lane = lax.broadcasted_iota(jnp.int32, (1, width), 1)
    live = [jnp.where(lane < counts[side], rows[side : side + 1, :], -1) for side in range(sides)]

    def build(step, _):
        start = pl.multiple_of(step * tile, tile)
        index = lax.broadcasted_iota(jnp.int32, (tile, width), 0) + start
        for side in range(sides):
            cols = slice(side * width, (side + 1) * width)
            pick_ref[pl.ds(start, tile), cols] = (index == live[side]).astype(F32).astype(BF16)
        index = lax.broadcasted_iota(jnp.int32, (tile, lanes), 0) + start
        corner_ref[pl.ds(start, tile), :] = (index == corners[...]).astype(F32).astype(BF16)
        return 0

    lax.fori_loop(0, unknowns // tile, build, 0)
    eye = lax.broadcasted_iota(jnp.int32, (tile, tile), 0) == lax.broadcasted_iota(
        jnp.int32, (tile, tile), 1
    )
    for part, copy in enumerate(copies):
        copy.wait()
        block = blocks[part].astype(F32)
        diag = jnp.sum(jnp.where(eye, block, 0.0), axis=0, keepdims=True)
        inv_ref[:, part * tile : (part + 1) * tile] = 1.0 / diag
    picked = mm(loads[...], corner_ref[...])
    cases = picked.shape[0]
    own, total = coarse.shape
    for peer in range(send_ref.shape[0]):
        send_ref[peer, :cases, :] = picked
        for part in range(total // lanes):
            send_ref[peer, cases + part * own : cases + (part + 1) * own, :] = coarse[
                :, part * lanes : (part + 1) * lanes
            ]
        send_ref[peer, cases + own * (total // lanes) :, :] = jnp.broadcast_to(
            slots[...].astype(F32), (8, lanes)
        )


def lift_kernel(slots, got, lift_ref, *, cases, own):
    peers, _, lanes = got.shape
    total = own * peers
    parts = total // lanes
    index = lax.broadcasted_iota(jnp.int32, (total, lanes), 0)
    mine = (index == slots[...]).astype(F32).astype(BF16)
    inverse = jnp.concatenate(
        [
            jnp.concatenate(
                [got[p, cases + q * own : cases + (q + 1) * own, :] for q in range(parts)], axis=1
            )
            for p in range(peers)
        ],
        axis=0,
    )
    high = inverse.astype(BF16)
    rest = inverse - high.astype(F32)
    middle, low = halves(rest)
    cols = (mm(high, mine) + mm(middle, mine)) + mm(low, mine)
    cols = jnp.concatenate(halves(cols), axis=1)
    base = cases + own * parts
    for peer in range(peers):
        theirs = got[peer, base : base + 1, :].astype(jnp.int32)
        theirs = (index == theirs).astype(F32).astype(BF16)
        lift_ref[peer * lanes : (peer + 1) * lanes, :] = mm(theirs, cols, TN).astype(BF16)


def corner_part(got, lift, cases, lanes):
    peers = got.shape[0]
    corners = jnp.concatenate([got[p, :cases, :] for p in range(peers)], axis=1)
    product = mm(stacked(corners), lift[...])
    return stacked(folded(product[:, :lanes]) + product[:cases, lanes:])


def begin_kernel(got, lift, corner, pick, loads, inv, field_ref, *send_refs):
    cases, unknowns = loads.shape
    back = corner_part(got, lift, cases, corner.shape[1])
    width = unknowns // 4
    for side in range(4):
        cols = slice(side * width, (side + 1) * width)
        added = folded(mm(back, corner[cols, :], NT))
        field_ref[:, cols] = stacked(loads[:, cols].astype(F32) * inv[:, cols] + added)
    for pair in range(2):
        cols = slice(2 * pair * width, 2 * (pair + 1) * width)
        sent = folded(mm(field_ref[...], pick[:, cols]))
        send_refs[2 * pair][...] = sent[:, :width]
        send_refs[2 * pair + 1][...] = sent[:, width:]


def lifted_kernel(
    got, lift, leave, ahead, inv_sent, from0, from1, from2, from3, back_ref, *send_refs
):
    cases = ahead.shape[0]
    back = corner_part(got, lift, cases, leave.shape[0])
    back_ref[...] = back
    width = ahead.shape[1] // 4
    for side, came in enumerate((from0, from1, from2, from3)):
        cols = slice(side * width, (side + 1) * width)
        value = ahead[:, cols] - came[...] * inv_sent[:, cols]
        send_refs[side][...] = value + folded(mm(back, leave[:, cols]))


def gram_slot(row, col):
    return col * (col + 1) // 2 + row + 5 if row >= 0 else col


def put(total, slot, value):
    lane = lax.broadcasted_iota(jnp.int32, total.shape, 1)
    return jnp.where(lane == slot, value, total)


def product(first, second):
    return jnp.sum(first * second, axis=1, keepdims=True)


def first_local_kernel(
    field, matrix, corner, pick, inv, loads,
    field_ref, acc_ref, local_ref, local_corner_ref, ahead_ref,
    arrive_ref, leave_ref, corner_matrix_ref, inv_sent_ref,
):
    cases, unknowns = loads.shape
    local = folded(mm(field[...], matrix[...]))
    local_ref[...] = local
    local_corner_ref[...] = folded(mm(stacked(local), corner[...]))
    value = field[:cases, :].astype(F32) + field[cases:, :].astype(F32)
    field_ref[...] = value
    total = jnp.zeros(acc_ref.shape, F32)
    acc_ref[...] = put(total, gram_slot(-1, 0), product(value, loads[...].astype(F32)))
    scale = jnp.broadcast_to(inv[...], (8, unknowns))
    high = scale.astype(BF16).astype(F32)
    middle = (scale - high).astype(BF16).astype(F32)
    pieces = jnp.concatenate(
        [high, middle, scale - high - middle, jnp.zeros_like(scale)], axis=0
    ).astype(BF16)
    left = jnp.concatenate([stacked(local * inv[...]), pieces], axis=0)
    wide = unknowns // 4
    for start in range(0, unknowns, wide):
        cols = slice(start, start + wide)
        picked = mm(left, pick[:, cols])
        ahead_ref[:, cols] = folded(picked[: 2 * cases])
        parts = picked[2 * cases :]
        inv_sent_ref[:, cols] = parts[0:1] + parts[8:9] + parts[16:17]
        arrive_ref[cols, :] = mm(pick[:, cols], corner[...], TN).astype(BF16)
        leave_ref[:, cols] = mm(corner[...], pick[:, cols], TN).astype(BF16)
        corner_matrix_ref[:, cols] = mm(corner[...], matrix[:, cols], TN).astype(BF16)


def local_kernel(*refs, step):
    from0, from1, from2, from3, back, before, local_before = refs[:7]
    matrix, corner, corner_matrix, pick, inv, loads, acc = refs[7:14]
    images = refs[14 : 13 + step]
    outs = refs[13 + step : -2]
    joined, scaled = refs[-2:]
    last = step == ITERS - 1
    cases, unknowns = loads.shape
    image_ref, field_ref, acc_ref = outs[:3]
    width = from0.shape[1]
    for side, came in enumerate((from0, from1, from2, from3)):
        joined[:, side * width : (side + 1) * width] = stacked(came[...])
    chunk = 512
    for start in range(0, unknowns, chunk):
        cols = slice(start, start + chunk)
        image = local_before[:, cols] - folded(mm(joined[...], pick[cols, :], NT))
        image_ref[:, cols] = image
        scaled[:, cols] = stacked(image * inv[:, cols])
    added = folded(mm(back[...], corner[...], NT))
    value = scaled[:cases, :].astype(F32) + scaled[cases:, :].astype(F32) + added
    field_ref[...] = value
    local = folded(mm(scaled[...], matrix[...])) + folded(mm(back[...], corner_matrix[...]))
    total = put(acc[...], gram_slot(-1, step), product(value, loads[...].astype(F32)))
    for row in range(step):
        image = image_ref if row == step - 1 else images[row]
        total = put(total, gram_slot(row, step), product(value, image[...]))
    total = put(total, gram_slot(step - 1, step - 1), product(before[...], image_ref[...]))
    if last:
        total = put(total, gram_slot(step, step), product(value, local))
    else:
        local_ref, local_corner_ref, ahead_ref = outs[3:]
        local_ref[...] = local
        local_corner_ref[...] = folded(mm(stacked(local), corner[...]))
        scaled[...] = stacked(local * inv[...])
        half = unknowns // 2
        for start in (0, half):
            cols = slice(start, start + half)
            ahead_ref[:, cols] = folded(mm(scaled[...], pick[:, cols]))
    acc_ref[...] = total


def corner_kernel(from0, from1, from2, from3, arrive, local_corner, send_ref):
    width = from0.shape[1]
    total = local_corner[...]
    for side, came in enumerate((from0, from1, from2, from3)):
        rows = slice(side * width, (side + 1) * width)
        total = total - folded(mm(stacked(came[...]), arrive[rows, :]))
    for peer in range(send_ref.shape[0]):
        send_ref[peer] = total


def gram_kernel(acc, sent0, from0, sent2, from2, send_ref):
    total = acc[...]
    lane = lax.broadcasted_iota(jnp.int32, total.shape, 1)
    pairs = sent0[...] * from0[...] + sent2[...] * from2[...]
    coupled = 2.0 * jnp.sum(pairs, axis=1, keepdims=True)
    slot = gram_slot(ITERS - 1, ITERS - 1)
    total = jnp.where(lane == slot, total - coupled, total).T
    packed = jnp.concatenate([total[:GRAM_ROWS], total[GRAM_ROWS : 2 * GRAM_ROWS]], axis=1)
    for peer in range(send_ref.shape[0]):
        send_ref[peer] = packed


def tree_sum(parts):
    while len(parts) > 1:
        parts = [a + b for a, b in zip(parts[::2], parts[1::2])] + parts[len(parts) & ~1 :]
    return parts[0]


def relay_kernel(got, send_ref):
    total = tree_sum([got[p] for p in range(got.shape[0])])
    for peer in range(send_ref.shape[0]):
        send_ref[peer] = total


def solve_kernel(got, *refs):
    fields = refs[:ITERS]
    out_ref, fault_ref = refs[ITERS:]
    total = tree_sum([got[p] for p in range(got.shape[0])])
    cases = out_ref.shape[0]

    def entry(row, col):
        slot = gram_slot(row, col)
        half, at = divmod(slot, GRAM_ROWS)
        return total[at : at + 1, half * cases : (half + 1) * cases]

    n = ITERS
    scale = [lax.rsqrt(entry(k, k)) for k in range(n)]
    rhs = [entry(-1, k) * scale[k] for k in range(n)]
    lower, pivots, solved = {}, [], []
    fault = jnp.zeros_like(rhs[0])
    for k in range(n):
        for j in range(k):
            value = (entry(j, k) * scale[j]) * scale[k]
            for m in range(j):
                value = value - (lower[k, m] * pivots[m]) * lower[j, m]
            lower[k, j] = value / pivots[j]
        pivot = jnp.ones_like(rhs[0])
        value = rhs[k]
        for m in range(k):
            pivot = pivot - (lower[k, m] * pivots[m]) * lower[k, m]
            value = value - lower[k, m] * solved[m]
        pivots.append(pivot)
        solved.append(value)
        good = (pivot > PIVOT_FLOOR) & (scale[k] > 0.0) & (scale[k] < 1e30)
        fault = jnp.maximum(fault, jnp.where(good, 0.0, 1.0))
    coeffs = [solved[k] / pivots[k] for k in range(n)]
    for k in reversed(range(n)):
        for m in range(k + 1, n):
            coeffs[k] = coeffs[k] - lower[m, k] * coeffs[m]
    coeffs = [coeffs[k] * scale[k] for k in range(n)]
    for k in range(n):
        good = jnp.abs(coeffs[k]) < 1e37
        fault = jnp.maximum(fault, jnp.where(good, 0.0, 1.0))
    fault_ref[0, 0] = jnp.max(fault)
    spread = jnp.concatenate(coeffs + [jnp.zeros_like(coeffs[0])] * (8 - n), axis=0)
    spread = jnp.concatenate([spread, jnp.zeros_like(spread)], axis=1).T[:cases]
    width = out_ref.shape[1] // 4
    for part in range(4):
        cols = slice(part * width, (part + 1) * width)
        value = spread[:, 0:1] * fields[0][:, cols]
        for k in range(1, n):
            value = value + spread[:, k : k + 1] * fields[k][:, cols]
        out_ref[:, cols] = value.astype(BF16)


def shifted(value, axis, shift, wrap):
    count = lax.axis_size(axis)
    pairs = [(i, (i + shift) % count) for i in range(count) if wrap or 0 <= i + shift < count]
    return lax.ppermute(value, axis, pairs)


def exchange(send, axis, groups=None):
    return lax.all_to_all(send, axis, 0, 0, axis_index_groups=groups)


def sum_groups(span, chord, inner):
    outer = span // inner
    first = [
        [(o * inner + i) * chord + c for o in range(outer) for c in range(chord)]
        for i in range(inner)
    ]
    second = [[o * inner + i for i in range(inner)] for o in range(outer)]
    return first, second


def shards(schur, loads, interface_rows, edge_rows, corner_rows, corner_map, coarse_inverse):
    originals = (
        schur, loads, interface_rows, edge_rows, corner_rows, corner_map, coarse_inverse
    )
    span, chord = lax.axis_size("span"), lax.axis_size("chord")
    matrix, rhs, block = schur[0, 0], loads[0, 0], coarse_inverse[0]
    unknowns = matrix.shape[0]
    cases = rhs.shape[0]
    rows, counts = interface_rows[0, 0], edge_rows[0, 0]
    width = rows.shape[1]
    lanes = corner_rows.shape[2]
    own, total = block.shape
    slots = corner_map[0]

    tile = 128
    pick, corner, inv, send = pl.pallas_call(
        setup_kernel,
        in_specs=[pl.BlockSpec(memory_space=pltpu.SMEM), pl.BlockSpec(memory_space=pl.ANY)]
        + [pl.BlockSpec(memory_space=pltpu.VMEM)] * 5,
        out_shape=(
            shape((unknowns, unknowns), BF16),
            shape((unknowns, lanes), BF16),
            shape((1, unknowns), F32),
            shape((chord, cases + own * (total // lanes) + 8, lanes), F32),
        ),
        scratch_shapes=[
            pltpu.VMEM((unknowns // tile, tile, tile), BF16),
            pltpu.SemaphoreType.DMA((unknowns // tile,)),
        ],
        compiler_params=pltpu.CompilerParams(vmem_limit_bytes=28 * 2**20),
    )(counts, matrix, rhs, rows, corner_rows[0], slots, block)
    got = exchange(send, "chord")
    lift = call(
        functools.partial(lift_kernel, cases=cases, own=own),
        shape((chord * lanes, 2 * lanes), BF16),
    )(slots, got)

    full = shape((cases, unknowns), F32)
    edges = (shape((cases, width), F32),) * 4
    table = shape((cases, 128), F32)
    corners = shape((cases, lanes), F32)
    doubled = shape((2 * cases, unknowns), BF16)
    fields, images = [], []
    for step in range(ITERS):
        last = step == ITERS - 1
        if step == 0:
            first, *sends = call(begin_kernel, (doubled, *edges))(
                got, lift, corner, pick, rhs, inv
            )
        else:
            back, *sends = call(lifted_kernel, (shape((2 * cases, lanes), BF16), *edges))(
                got, lift, leave, ahead, inv_sent, *came
            )
        earlier = came if step else ()
        came = [
            shifted(sends[1], "span", 1, False),
            None if last else shifted(sends[0], "span", -1, False),
            shifted(sends[3], "chord", 1, True),
            None if last else shifted(sends[2], "chord", -1, True),
        ]
        if step == 0:
            field, acc, local, local_corner, ahead, arrive, leave, corner_matrix, inv_sent = call(
                first_local_kernel,
                (
                    full, table, full, corners, full,
                    shape((unknowns, lanes), BF16),
                    shape((lanes, unknowns), BF16),
                    shape((lanes, unknowns), BF16),
                    shape((1, unknowns), F32),
                ),
                flops=10**9,
            )(first, matrix, corner, pick, inv, rhs)
        else:
            image, field, acc, *rest = call(
                functools.partial(local_kernel, step=step),
                (full, full, table) + (() if last else (full, corners, full)),
                scratch=[pltpu.VMEM(doubled.shape, BF16)] * 2,
                flops=10**9,
            )(
                *earlier, back, fields[-1], local,
                matrix, corner, corner_matrix, pick, inv, rhs, acc, *images,
            )
            images.append(image)
            if not last:
                local, local_corner, ahead = rest
        fields.append(field)
        if not last:
            send = call(corner_kernel, shape((chord, cases, lanes), F32))(
                *came, arrive, local_corner
            )
            got = exchange(send, "chord")

    inner = 16 if span % 16 == 0 else span
    first, second = sum_groups(span, chord, inner)
    send = call(gram_kernel, shape((len(first[0]), GRAM_ROWS, 128), F32))(
        acc, sends[0], came[0], sends[2], came[2]
    )
    got = exchange(send, ("span", "chord"), first)
    send = call(relay_kernel, shape((inner, GRAM_ROWS, 128), F32))(got)
    got = exchange(send, "span", second)
    answer, fault = pl.pallas_call(
        solve_kernel,
        out_shape=(shape((cases, unknowns), BF16), shape((1, 1), F32)),
        out_specs=(
            pl.BlockSpec(memory_space=pltpu.VMEM),
            pl.BlockSpec(memory_space=pltpu.SMEM),
        ),
        compiler_params=pltpu.CompilerParams(vmem_limit_bytes=28 * 2**20),
    )(got, *fields)
    answer = lax.cond(
        fault[0, 0] > 0.0,
        lambda answer, *arrays: plain_recurrence(*arrays),
        lambda answer, *arrays: answer,
        answer,
        *originals,
    )
    return answer[None, None]


def solution(mesh):
    return jax.shard_map(
        shards,
        mesh=mesh,
        in_specs=(
            P("span", "chord", None, None),
            P("span", "chord", None, None),
            P("span", "chord", None, None),
            P("span", "chord", None),
            P("span", "chord", None),
            P("span", "chord", None),
            P("span", "chord", None),
        ),
        out_specs=P("span", "chord", None, None),
        check_vma=False,
    )
```

```python
import functools

import jax
import jax.numpy as jnp
from jax import lax
from jax.experimental import pallas as pl
from jax.experimental.pallas import tpu as pltpu
from jax.sharding import PartitionSpec as P

ITERS = 5
F32 = jnp.float32
BF16 = jnp.bfloat16
PIVOT_FLOOR = 2e-5
GRAM_ROWS = 8


def with_halo(block, sides, width):
    for axis, dim in sides:
        count = lax.axis_size(axis)
        forward = [(i, i + 1) for i in range(count - 1)]
        backward = [(target, source) for source, target in forward]
        low = lax.ppermute(
            lax.slice_in_dim(block, block.shape[dim] - width, None, axis=dim), axis, forward
        )
        high = lax.ppermute(lax.slice_in_dim(block, 0, width, axis=dim), axis, backward)
        block = jnp.concatenate([low, block, high], axis=dim)
    return block


def case_sum(first, second):
    return lax.psum(jnp.sum(first * second, axis=1), ("span", "chord"))


def plain_recurrence(
    schur, loads, interface_rows, edge_rows, corner_rows, corner_map, coarse_inverse
):
    matrix = schur[0, 0]
    rows = interface_rows[0, 0]
    counts = edge_rows[0, 0]
    corners = corner_rows[0, 0]
    block = coarse_inverse[0]
    width = rows.shape[1]
    unknowns = matrix.shape[0]
    total_rows = block.shape[1]
    live = (jnp.arange(width, dtype=jnp.int32)[None, :] < counts[:, None]).astype(BF16)
    flat_rows = rows.reshape(-1)
    inv_diag = 1.0 / jnp.diagonal(matrix).astype(F32)
    onehot = (
        corner_map[0, 0][:, None] == jnp.arange(total_rows, dtype=jnp.int32)[None, :]
    ).astype(F32)
    highest = lax.Precision.HIGHEST

    def precondition(resid):
        term = jnp.dot(resid[:, corners], onehot, precision=highest)
        summed = lax.psum(term, "chord")
        own_rows = jnp.dot(summed, block.T, precision=highest)
        lifted = lax.all_gather(own_rows, "chord", axis=1, tiled=True)
        back = jnp.dot(lifted, onehot.T, precision=highest)
        return (resid * inv_diag[None, :]).at[:, corners].add(back)

    def apply_operator(direction):
        rounded = direction.astype(BF16)
        picks = [rounded[:, rows[side]] * live[side][None, :] for side in range(4)]
        span_ext = with_halo(jnp.stack([picks[0], picks[1]]), (("span", 0),), 1)
        chord_ext = with_halo(jnp.stack([picks[2], picks[3]]), (("chord", 0),), 1)
        local = jnp.dot(rounded, matrix, preferred_element_type=F32)
        arrived = jnp.concatenate([span_ext[0], span_ext[3], chord_ext[0], chord_ext[3]], axis=1)
        coupled = (
            jnp.zeros((direction.shape[0], unknowns), F32)
            .at[:, flat_rows]
            .add(arrived.astype(F32))
        )
        return local - coupled

    resid = loads[0, 0].astype(F32)
    result = jnp.zeros_like(resid)
    direction = precondition(resid)
    norm_now = case_sum(resid, direction)

    def step(_, carry):
        result, resid, direction, norm_now = carry
        image = apply_operator(direction)
        alpha = norm_now / case_sum(direction, image)
        result = result + alpha[:, None] * direction
        resid = resid - alpha[:, None] * image
        precond = precondition(resid)
        norm_next = case_sum(resid, precond)
        direction = precond + (norm_next / norm_now)[:, None] * direction
        return result, resid, direction, norm_next

    result, resid, direction, norm_now = lax.fori_loop(
        0, ITERS - 1, step, (result, resid, direction, norm_now)
    )
    alpha = norm_now / case_sum(direction, apply_operator(direction))
    return (result + alpha[:, None] * direction).astype(BF16)


NN = (((1,), (0,)), ((), ()))
NT = (((1,), (1,)), ((), ()))
TN = (((0,), (0,)), ((), ()))


def mm(first, second, dims=NN):
    return lax.dot_general(first, second, dims, preferred_element_type=F32)


def halves(value):
    high = value.astype(BF16)
    return high, (value - high.astype(F32)).astype(BF16)


def stacked(value):
    return jnp.concatenate(halves(value), axis=0)


def folded(value):
    half = value.shape[0] // 2
    return value[:half] + value[half:]


def call(body, outs, scratch=(), limit=28, flops=10**8):
    return pl.pallas_call(
        body,
        out_shape=outs,
        scratch_shapes=list(scratch),
        compiler_params=pltpu.CompilerParams(vmem_limit_bytes=limit * 2**20),
        cost_estimate=pl.CostEstimate(flops=flops, bytes_accessed=10**6, transcendentals=0),
    )


def shape(dims, dtype):
    return jax.ShapeDtypeStruct(dims, dtype)


def setup_kernel(
    counts, turn_ref, schur, loads, rows, corners, slots, coarse,
    pick_ref, corner_ref, inv_ref, send_ref, blocks, sems,
):
    unknowns = loads.shape[1]
    lanes = corners.shape[1]
    tile = blocks.shape[1]
    copies = []
    for part in range(unknowns // tile):
        span = pl.ds(part * tile, tile)
        copy = pltpu.make_async_copy(schur.at[span, span], blocks.at[part], sems.at[part])
        copy.start()
        copies.append(copy)

    sides, width = rows.shape
    lane = lax.broadcasted_iota(jnp.int32, (1, width), 1)
    live = [jnp.where(lane < counts[side], rows[side : side + 1, :], -1) for side in range(sides)]

    def build(step, _):
        start = pl.multiple_of(step * tile, tile)
        index = lax.broadcasted_iota(jnp.int32, (tile, width), 0) + start
        for side in range(sides):
            cols = slice(side * width, (side + 1) * width)
            pick_ref[pl.ds(start, tile), cols] = (index == live[side]).astype(F32).astype(BF16)
        index = lax.broadcasted_iota(jnp.int32, (tile, lanes), 0) + start
        corner_ref[pl.ds(start, tile), :] = (index == corners[...]).astype(F32).astype(BF16)
        return 0

    lax.fori_loop(0, unknowns // tile, build, 0)
    eye = lax.broadcasted_iota(jnp.int32, (tile, tile), 0) == lax.broadcasted_iota(
        jnp.int32, (tile, tile), 1
    )
    for part, copy in enumerate(copies):
        copy.wait()
        block = blocks[part].astype(F32)
        diag = jnp.sum(jnp.where(eye, block, 0.0), axis=0, keepdims=True)
        inv_ref[:, part * tile : (part + 1) * tile] = 1.0 / diag
    picked = mm(loads[...], corner_ref[...])
    cases = picked.shape[0]
    own, total = coarse.shape
    parts = (send_ref.shape[1] - cases - 8) // own
    turned = pltpu.roll(coarse[...], turn_ref[0], 1)
    for peer in range(send_ref.shape[0]):
        send_ref[peer, :cases, :] = picked
        for part in range(parts):
            send_ref[peer, cases + part * own : cases + (part + 1) * own, :] = turned[
                :, part * lanes : (part + 1) * lanes
            ]
        send_ref[peer, cases + own * parts :, :] = jnp.broadcast_to(
            slots[...].astype(F32), (8, lanes)
        )


def coarse_parts(own, peers, lanes):
    return -(-own * (peers // 2 + 1) // lanes)


def lift_kernel(slots, got, lift_ref, *, cases, own):
    peers, _, lanes = got.shape
    total = own * peers
    parts = coarse_parts(own, peers, lanes)
    index = lax.broadcasted_iota(jnp.int32, (total, lanes), 0)
    mine = (index == slots[...]).astype(F32).astype(BF16)
    lane = lax.broadcasted_iota(jnp.int32, (own, total), 1)
    reach = own * (peers // 2)
    weight = jnp.where((lane < own) | (lane >= reach), 0.5, 1.0)
    weight = jnp.where(lane < reach + own, weight, 0.0)
    rows = []
    for p in range(peers):
        pieces = [got[p, cases + q * own : cases + (q + 1) * own, :] for q in range(parts)]
        pieces += [jnp.zeros((own, lanes), F32)] * (total // lanes - parts)
        row = jnp.concatenate(pieces, axis=1) * weight
        rows.append(pltpu.roll(row, p * own, 1) if p else row)
    half = jnp.concatenate(rows, axis=0)
    inverse = half + half.T
    high = inverse.astype(BF16)
    rest = inverse - high.astype(F32)
    middle, low = halves(rest)
    cols = (mm(high, mine) + mm(middle, mine)) + mm(low, mine)
    cols = jnp.concatenate(halves(cols), axis=1)
    base = cases + own * parts
    for peer in range(peers):
        theirs = got[peer, base : base + 1, :].astype(jnp.int32)
        theirs = (index == theirs).astype(F32).astype(BF16)
        lift_ref[peer * lanes : (peer + 1) * lanes, :] = mm(theirs, cols, TN).astype(BF16)


def corner_part(got, lift, cases, lanes):
    peers = got.shape[0]
    corners = jnp.concatenate([got[p, :cases, :] for p in range(peers)], axis=1)
    product = mm(stacked(corners), lift[...])
    return stacked(folded(product[:, :lanes]) + product[:cases, lanes:])


def begin_kernel(got, lift, corner, pick, loads, inv, field_ref, *send_refs):
    cases, unknowns = loads.shape
    back = corner_part(got, lift, cases, corner.shape[1])
    width = unknowns // 4
    for side in range(4):
        cols = slice(side * width, (side + 1) * width)
        added = folded(mm(back, corner[cols, :], NT))
        field_ref[:, cols] = stacked(loads[:, cols].astype(F32) * inv[:, cols] + added)
    for pair in range(2):
        cols = slice(2 * pair * width, 2 * (pair + 1) * width)
        sent = folded(mm(field_ref[...], pick[:, cols]))
        send_refs[2 * pair][...] = sent[:, :width]
        send_refs[2 * pair + 1][...] = sent[:, width:]


def lifted_kernel(
    got, lift, leave, ahead, inv_sent, from0, from1, from2, from3, back_ref, *send_refs
):
    cases = ahead.shape[0]
    back = corner_part(got, lift, cases, leave.shape[0])
    back_ref[...] = back
    width = ahead.shape[1] // 4
    for side, came in enumerate((from0, from1, from2, from3)):
        cols = slice(side * width, (side + 1) * width)
        value = ahead[:, cols] - came[...] * inv_sent[:, cols]
        send_refs[side][...] = value + folded(mm(back, leave[:, cols]))


def gram_slot(row, col):
    if row < 0:
        return 0 if col == 0 else gram_slot(0, col - 1)
    return col * (col + 1) // 2 + row + 1


def put(total, slot, value):
    lane = lax.broadcasted_iota(jnp.int32, total.shape, 1)
    return jnp.where(lane == slot, value, total)


def product(first, second):
    return jnp.sum(first * second, axis=1, keepdims=True)


def first_local_kernel(
    field, matrix, corner, pick, inv, loads,
    field_ref, acc_ref, local_ref, local_corner_ref, ahead_ref,
    leave_ref, corner_matrix_ref, inv_sent_ref,
):
    cases, unknowns = loads.shape
    local = folded(mm(field[...], matrix[...]))
    local_ref[...] = local
    local_corner_ref[...] = folded(mm(stacked(local), corner[...]))
    value = field[:cases, :].astype(F32) + field[cases:, :].astype(F32)
    field_ref[...] = value
    total = jnp.zeros(acc_ref.shape, F32)
    acc_ref[...] = put(total, gram_slot(-1, 0), product(value, loads[...].astype(F32)))
    scale = jnp.broadcast_to(inv[...], (8, unknowns))
    high = scale.astype(BF16).astype(F32)
    middle = (scale - high).astype(BF16).astype(F32)
    pieces = jnp.concatenate(
        [high, middle, scale - high - middle, jnp.zeros_like(scale)], axis=0
    ).astype(BF16)
    left = jnp.concatenate([stacked(local * inv[...]), pieces], axis=0)
    wide = unknowns // 4
    for start in range(0, unknowns, wide):
        cols = slice(start, start + wide)
        picked = mm(left, pick[:, cols])
        ahead_ref[:, cols] = folded(picked[: 2 * cases])
        parts = picked[2 * cases :]
        inv_sent_ref[:, cols] = parts[0:1] + parts[8:9] + parts[16:17]
        leave_ref[:, cols] = mm(corner[...], pick[:, cols], TN).astype(BF16)
        corner_matrix_ref[:, cols] = mm(corner[...], matrix[:, cols], TN).astype(BF16)


def local_kernel(*refs, step):
    from0, from1, from2, from3, back, before, local_before = refs[:7]
    matrix, corner, corner_matrix, pick, inv, loads, acc = refs[7:14]
    images = refs[14 : 13 + step]
    outs = refs[13 + step : -2]
    joined, scaled = refs[-2:]
    last = step == ITERS - 1
    cases, unknowns = loads.shape
    image_ref, field_ref, acc_ref = outs[:3]
    width = from0.shape[1]
    for side, came in enumerate((from0, from1, from2, from3)):
        joined[:, side * width : (side + 1) * width] = stacked(came[...])
    chunk = 512
    for start in range(0, unknowns, chunk):
        cols = slice(start, start + chunk)
        image = local_before[:, cols] - folded(mm(joined[...], pick[cols, :], NT))
        image_ref[:, cols] = image
        scaled[:, cols] = stacked(image * inv[:, cols])
    added = folded(mm(back[...], corner[...], NT))
    value = scaled[:cases, :].astype(F32) + scaled[cases:, :].astype(F32) + added
    field_ref[...] = value
    local = folded(mm(scaled[...], matrix[...])) + folded(mm(back[...], corner_matrix[...]))
    total = acc[...]
    for row in range(step):
        image = image_ref if row == step - 1 else images[row]
        total = put(total, gram_slot(row, step), product(value, image[...]))
    total = put(total, gram_slot(step - 1, step - 1), product(before[...], image_ref[...]))
    if last:
        total = put(total, gram_slot(step, step), product(value, local))
    else:
        local_ref, local_corner_ref, ahead_ref = outs[3:]
        local_ref[...] = local
        local_corner_ref[...] = folded(mm(stacked(local), corner[...]))
        scaled[...] = stacked(local * inv[...])
        half = unknowns // 2
        for start in (0, half):
            cols = slice(start, start + half)
            ahead_ref[:, cols] = folded(mm(scaled[...], pick[:, cols]))
    acc_ref[...] = total


def corner_kernel(from0, from1, from2, from3, leave, local_corner, send_ref):
    width = from0.shape[1]
    total = local_corner[...]
    for side, came in enumerate((from0, from1, from2, from3)):
        cols = slice(side * width, (side + 1) * width)
        total = total - folded(mm(stacked(came[...]), leave[:, cols], NT))
    for peer in range(send_ref.shape[0]):
        send_ref[peer] = total


def gram_kernel(acc, sent0, from0, sent2, from2, send_ref):
    total = acc[...]
    lane = lax.broadcasted_iota(jnp.int32, total.shape, 1)
    pairs = sent0[...] * from0[...] + sent2[...] * from2[...]
    coupled = 2.0 * jnp.sum(pairs, axis=1, keepdims=True)
    slot = gram_slot(ITERS - 1, ITERS - 1)
    total = jnp.where(lane == slot, total - coupled, total).T
    packed = jnp.concatenate([total[:GRAM_ROWS], total[GRAM_ROWS : 2 * GRAM_ROWS]], axis=1)
    for peer in range(send_ref.shape[0]):
        send_ref[peer] = packed


def tree_sum(parts):
    while len(parts) > 1:
        parts = [a + b for a, b in zip(parts[::2], parts[1::2])] + parts[len(parts) & ~1 :]
    return parts[0]


def relay_kernel(got, send_ref):
    total = tree_sum([got[p] for p in range(got.shape[0])])
    for peer in range(send_ref.shape[0]):
        send_ref[peer] = total


def solve_kernel(got, *refs):
    fields = refs[:ITERS]
    out_ref, fault_ref = refs[ITERS:]
    total = tree_sum([got[p] for p in range(got.shape[0])])
    cases = out_ref.shape[0]

    def entry(row, col):
        slot = gram_slot(row, col)
        half, at = divmod(slot, GRAM_ROWS)
        return total[at : at + 1, half * cases : (half + 1) * cases]

    n = ITERS
    scale = [lax.rsqrt(entry(k, k)) for k in range(n)]
    rhs = [entry(-1, k) * scale[k] for k in range(n)]
    lower, pivots, solved = {}, [], []
    fault = jnp.zeros_like(rhs[0])
    for k in range(n):
        for j in range(k):
            value = (entry(j, k) * scale[j]) * scale[k]
            for m in range(j):
                value = value - (lower[k, m] * pivots[m]) * lower[j, m]
            lower[k, j] = value / pivots[j]
        pivot = jnp.ones_like(rhs[0])
        value = rhs[k]
        for m in range(k):
            pivot = pivot - (lower[k, m] * pivots[m]) * lower[k, m]
            value = value - lower[k, m] * solved[m]
        pivots.append(pivot)
        solved.append(value)
        good = (pivot > PIVOT_FLOOR) & (scale[k] > 0.0) & (scale[k] < 1e30)
        fault = jnp.maximum(fault, jnp.where(good, 0.0, 1.0))
    coeffs = [solved[k] / pivots[k] for k in range(n)]
    for k in reversed(range(n)):
        for m in range(k + 1, n):
            coeffs[k] = coeffs[k] - lower[m, k] * coeffs[m]
    coeffs = [coeffs[k] * scale[k] for k in range(n)]
    for k in range(n):
        good = jnp.abs(coeffs[k]) < 1e37
        fault = jnp.maximum(fault, jnp.where(good, 0.0, 1.0))
    fault_ref[0, 0] = jnp.max(fault)
    spread = jnp.concatenate(coeffs + [jnp.zeros_like(coeffs[0])] * (8 - n), axis=0)
    spread = jnp.concatenate([spread, jnp.zeros_like(spread)], axis=1).T[:cases]
    width = out_ref.shape[1] // 4
    for part in range(4):
        cols = slice(part * width, (part + 1) * width)
        value = spread[:, 0:1] * fields[0][:, cols]
        for k in range(1, n):
            value = value + spread[:, k : k + 1] * fields[k][:, cols]
        out_ref[:, cols] = value.astype(BF16)


def shifted(value, axis, shift, wrap):
    count = lax.axis_size(axis)
    pairs = [(i, (i + shift) % count) for i in range(count) if wrap or 0 <= i + shift < count]
    return lax.ppermute(value, axis, pairs)


def exchange(send, axis, groups=None):
    return lax.all_to_all(send, axis, 0, 0, axis_index_groups=groups)


def sum_groups(span, chord, inner):
    outer = span // inner
    first = [
        [(o * inner + i) * chord + c for o in range(outer) for c in range(chord)]
        for i in range(inner)
    ]
    second = [[o * inner + i for i in range(inner)] for o in range(outer)]
    return first, second


def shards(schur, loads, interface_rows, edge_rows, corner_rows, corner_map, coarse_inverse):
    originals = (
        schur, loads, interface_rows, edge_rows, corner_rows, corner_map, coarse_inverse
    )
    span, chord = lax.axis_size("span"), lax.axis_size("chord")
    matrix, rhs, block = schur[0, 0], loads[0, 0], coarse_inverse[0]
    unknowns = matrix.shape[0]
    cases = rhs.shape[0]
    rows, counts = interface_rows[0, 0], edge_rows[0, 0]
    width = rows.shape[1]
    lanes = corner_rows.shape[2]
    own, total = block.shape
    slots = corner_map[0]

    tile = 128
    turn = lax.rem(total - lax.axis_index("chord") * own, total).astype(jnp.int32).reshape(1)
    pick, corner, inv, send = pl.pallas_call(
        setup_kernel,
        in_specs=[pl.BlockSpec(memory_space=pltpu.SMEM)] * 2
        + [pl.BlockSpec(memory_space=pl.ANY)]
        + [pl.BlockSpec(memory_space=pltpu.VMEM)] * 5,
        out_shape=(
            shape((unknowns, unknowns), BF16),
            shape((unknowns, lanes), BF16),
            shape((1, unknowns), F32),
            shape((chord, cases + own * coarse_parts(own, chord, lanes) + 8, lanes), F32),
        ),
        scratch_shapes=[
            pltpu.VMEM((unknowns // tile, tile, tile), BF16),
            pltpu.SemaphoreType.DMA((unknowns // tile,)),
        ],
        compiler_params=pltpu.CompilerParams(vmem_limit_bytes=28 * 2**20),
    )(counts, turn, matrix, rhs, rows, corner_rows[0], slots, block)
    got = exchange(send, "chord")
    lift = call(
        functools.partial(lift_kernel, cases=cases, own=own),
        shape((chord * lanes, 2 * lanes), BF16),
    )(slots, got)

    full = shape((cases, unknowns), F32)
    edges = (shape((cases, width), F32),) * 4
    table = shape((cases, 128), F32)
    corners = shape((cases, lanes), F32)
    doubled = shape((2 * cases, unknowns), BF16)
    fields, images = [], []
    for step in range(ITERS):
        last = step == ITERS - 1
        if step == 0:
            first, *sends = call(begin_kernel, (doubled, *edges))(
                got, lift, corner, pick, rhs, inv
            )
        else:
            back, *sends = call(lifted_kernel, (shape((2 * cases, lanes), BF16), *edges))(
                got, lift, leave, ahead, inv_sent, *came
            )
        earlier = came if step else ()
        came = [
            shifted(sends[1], "span", 1, False),
            None if last else shifted(sends[0], "span", -1, False),
            shifted(sends[3], "chord", 1, True),
            None if last else shifted(sends[2], "chord", -1, True),
        ]
        if step == 0:
            field, acc, local, local_corner, ahead, leave, corner_matrix, inv_sent = call(
                first_local_kernel,
                (
                    full, table, full, corners, full,
                    shape((lanes, unknowns), BF16),
                    shape((lanes, unknowns), BF16),
                    shape((1, unknowns), F32),
                ),
                flops=10**9,
            )(first, matrix, corner, pick, inv, rhs)
        else:
            image, field, acc, *rest = call(
                functools.partial(local_kernel, step=step),
                (full, full, table) + (() if last else (full, corners, full)),
                scratch=[pltpu.VMEM(doubled.shape, BF16)] * 2,
                flops=10**9,
            )(
                *earlier, back, fields[-1], local,
                matrix, corner, corner_matrix, pick, inv, rhs, acc, *images,
            )
            images.append(image)
            if not last:
                local, local_corner, ahead = rest
        fields.append(field)
        if not last:
            send = call(corner_kernel, shape((chord, cases, lanes), F32))(
                *came, leave, local_corner
            )
            got = exchange(send, "chord")

    inner = 16 if span % 16 == 0 else span
    first, second = sum_groups(span, chord, inner)
    send = call(gram_kernel, shape((len(first[0]), GRAM_ROWS, 128), F32))(
        acc, sends[0], came[0], sends[2], came[2]
    )
    got = exchange(send, ("span", "chord"), first)
    send = call(relay_kernel, shape((inner, GRAM_ROWS, 128), F32))(got)
    got = exchange(send, "span", second)
    answer, fault = pl.pallas_call(
        solve_kernel,
        out_shape=(shape((cases, unknowns), BF16), shape((1, 1), F32)),
        out_specs=(
            pl.BlockSpec(memory_space=pltpu.VMEM),
            pl.BlockSpec(memory_space=pltpu.SMEM),
        ),
        compiler_params=pltpu.CompilerParams(vmem_limit_bytes=28 * 2**20),
    )(got, *fields)
    answer = lax.cond(
        fault[0, 0] > 0.0,
        lambda answer, *arrays: plain_recurrence(*arrays),
        lambda answer, *arrays: answer,
        answer,
        *originals,
    )
    return answer[None, None]


def solution(mesh):
    return jax.shard_map(
        shards,
        mesh=mesh,
        in_specs=(
            P("span", "chord", None, None),
            P("span", "chord", None, None),
            P("span", "chord", None, None),
            P("span", "chord", None),
            P("span", "chord", None),
            P("span", "chord", None),
            P("span", "chord", None),
        ),
        out_specs=P("span", "chord", None, None),
        check_vma=False,
    )
```

```python
import functools

import jax
import jax.numpy as jnp
from jax import lax
from jax.experimental import pallas as pl
from jax.experimental.pallas import tpu as pltpu
from jax.sharding import PartitionSpec as P

ITERS = 5
F32 = jnp.float32
BF16 = jnp.bfloat16
PIVOT_FLOOR = 2e-5
NOISE_BOUND = 2.5e-4
ROUNDING = 1.2e-7
GRAM_ROWS = 8


def with_halo(block, sides, width):
    for axis, dim in sides:
        count = lax.axis_size(axis)
        forward = [(i, i + 1) for i in range(count - 1)]
        backward = [(target, source) for source, target in forward]
        low = lax.ppermute(
            lax.slice_in_dim(block, block.shape[dim] - width, None, axis=dim), axis, forward
        )
        high = lax.ppermute(lax.slice_in_dim(block, 0, width, axis=dim), axis, backward)
        block = jnp.concatenate([low, block, high], axis=dim)
    return block


def case_sum(first, second):
    return lax.psum(jnp.sum(first * second, axis=1), ("span", "chord"))


def plain_recurrence(
    schur, loads, interface_rows, edge_rows, corner_rows, corner_map, coarse_inverse
):
    matrix = schur[0, 0]
    rows = interface_rows[0, 0]
    counts = edge_rows[0, 0]
    corners = corner_rows[0, 0]
    block = coarse_inverse[0]
    width = rows.shape[1]
    unknowns = matrix.shape[0]
    total_rows = block.shape[1]
    live = (jnp.arange(width, dtype=jnp.int32)[None, :] < counts[:, None]).astype(BF16)
    flat_rows = rows.reshape(-1)
    inv_diag = 1.0 / jnp.diagonal(matrix).astype(F32)
    onehot = (
        corner_map[0, 0][:, None] == jnp.arange(total_rows, dtype=jnp.int32)[None, :]
    ).astype(F32)
    highest = lax.Precision.HIGHEST

    def precondition(resid):
        term = jnp.dot(resid[:, corners], onehot, precision=highest)
        summed = lax.psum(term, "chord")
        own_rows = jnp.dot(summed, block.T, precision=highest)
        lifted = lax.all_gather(own_rows, "chord", axis=1, tiled=True)
        back = jnp.dot(lifted, onehot.T, precision=highest)
        return (resid * inv_diag[None, :]).at[:, corners].add(back)

    def apply_operator(direction):
        rounded = direction.astype(BF16)
        picks = [rounded[:, rows[side]] * live[side][None, :] for side in range(4)]
        span_ext = with_halo(jnp.stack([picks[0], picks[1]]), (("span", 0),), 1)
        chord_ext = with_halo(jnp.stack([picks[2], picks[3]]), (("chord", 0),), 1)
        local = jnp.dot(rounded, matrix, preferred_element_type=F32)
        arrived = jnp.concatenate([span_ext[0], span_ext[3], chord_ext[0], chord_ext[3]], axis=1)
        coupled = (
            jnp.zeros((direction.shape[0], unknowns), F32)
            .at[:, flat_rows]
            .add(arrived.astype(F32))
        )
        return local - coupled

    resid = loads[0, 0].astype(F32)
    result = jnp.zeros_like(resid)
    direction = precondition(resid)
    norm_now = case_sum(resid, direction)

    def step(_, carry):
        result, resid, direction, norm_now = carry
        image = apply_operator(direction)
        alpha = norm_now / case_sum(direction, image)
        result = result + alpha[:, None] * direction
        resid = resid - alpha[:, None] * image
        precond = precondition(resid)
        norm_next = case_sum(resid, precond)
        direction = precond + (norm_next / norm_now)[:, None] * direction
        return result, resid, direction, norm_next

    result, resid, direction, norm_now = lax.fori_loop(
        0, ITERS - 1, step, (result, resid, direction, norm_now)
    )
    alpha = norm_now / case_sum(direction, apply_operator(direction))
    return (result + alpha[:, None] * direction).astype(BF16)


NN = (((1,), (0,)), ((), ()))
NT = (((1,), (1,)), ((), ()))
TN = (((0,), (0,)), ((), ()))


def mm(first, second, dims=NN):
    return lax.dot_general(first, second, dims, preferred_element_type=F32)


def halves(value):
    high = value.astype(BF16)
    return high, (value - high.astype(F32)).astype(BF16)


def stacked(value):
    return jnp.concatenate(halves(value), axis=0)


def folded(value):
    half = value.shape[0] // 2
    return value[:half] + value[half:]


def call(body, outs, scratch=(), limit=28, flops=10**8):
    return pl.pallas_call(
        body,
        out_shape=outs,
        scratch_shapes=list(scratch),
        compiler_params=pltpu.CompilerParams(vmem_limit_bytes=limit * 2**20),
        cost_estimate=pl.CostEstimate(flops=flops, bytes_accessed=10**6, transcendentals=0),
    )


def shape(dims, dtype):
    return jax.ShapeDtypeStruct(dims, dtype)


def setup_kernel(
    counts, turn_ref, schur, loads, rows, corners, slots, coarse,
    pick_ref, corner_ref, inv_ref, send_ref, blocks, sems,
):
    unknowns = loads.shape[1]
    lanes = corners.shape[1]
    tile = blocks.shape[1]
    copies = []
    for part in range(unknowns // tile):
        span = pl.ds(part * tile, tile)
        copy = pltpu.make_async_copy(schur.at[span, span], blocks.at[part], sems.at[part])
        copy.start()
        copies.append(copy)

    sides, width = rows.shape
    lane = lax.broadcasted_iota(jnp.int32, (1, width), 1)
    live = [jnp.where(lane < counts[side], rows[side : side + 1, :], -1) for side in range(sides)]

    def build(step, _):
        start = pl.multiple_of(step * tile, tile)
        index = lax.broadcasted_iota(jnp.int32, (tile, width), 0) + start
        for side in range(sides):
            cols = slice(side * width, (side + 1) * width)
            pick_ref[pl.ds(start, tile), cols] = (index == live[side]).astype(F32).astype(BF16)
        index = lax.broadcasted_iota(jnp.int32, (tile, lanes), 0) + start
        corner_ref[pl.ds(start, tile), :] = (index == corners[...]).astype(F32).astype(BF16)
        return 0

    lax.fori_loop(0, unknowns // tile, build, 0)
    eye = lax.broadcasted_iota(jnp.int32, (tile, tile), 0) == lax.broadcasted_iota(
        jnp.int32, (tile, tile), 1
    )
    for part, copy in enumerate(copies):
        copy.wait()
        block = blocks[part].astype(F32)
        diag = jnp.sum(jnp.where(eye, block, 0.0), axis=0, keepdims=True)
        inv_ref[:, part * tile : (part + 1) * tile] = 1.0 / diag
    picked = mm(loads[...], corner_ref[...])
    cases = picked.shape[0]
    own, total = coarse.shape
    parts = (send_ref.shape[1] - cases - 8) // own
    turned = pltpu.roll(coarse[...], turn_ref[0], 1)
    for peer in range(send_ref.shape[0]):
        send_ref[peer, :cases, :] = picked
        for part in range(parts):
            send_ref[peer, cases + part * own : cases + (part + 1) * own, :] = turned[
                :, part * lanes : (part + 1) * lanes
            ]
        send_ref[peer, cases + own * parts :, :] = jnp.broadcast_to(
            slots[...].astype(F32), (8, lanes)
        )


def coarse_parts(own, peers, lanes):
    return -(-own * (peers // 2 + 1) // lanes)


def lift_kernel(slots, got, lift_ref, *, cases, own):
    peers, _, lanes = got.shape
    total = own * peers
    parts = coarse_parts(own, peers, lanes)
    index = lax.broadcasted_iota(jnp.int32, (total, lanes), 0)
    mine = (index == slots[...]).astype(F32).astype(BF16)
    lane = lax.broadcasted_iota(jnp.int32, (own, total), 1)
    reach = own * (peers // 2)
    weight = jnp.where((lane < own) | (lane >= reach), 0.5, 1.0)
    weight = jnp.where(lane < reach + own, weight, 0.0)
    rows = []
    for p in range(peers):
        pieces = [got[p, cases + q * own : cases + (q + 1) * own, :] for q in range(parts)]
        pieces += [jnp.zeros((own, lanes), F32)] * (total // lanes - parts)
        row = jnp.concatenate(pieces, axis=1) * weight
        rows.append(pltpu.roll(row, p * own, 1) if p else row)
    half = jnp.concatenate(rows, axis=0)
    inverse = half + half.T
    high = inverse.astype(BF16)
    rest = inverse - high.astype(F32)
    middle, low = halves(rest)
    cols = (mm(high, mine) + mm(middle, mine)) + mm(low, mine)
    cols = jnp.concatenate(halves(cols), axis=1)
    base = cases + own * parts
    for peer in range(peers):
        theirs = got[peer, base : base + 1, :].astype(jnp.int32)
        theirs = (index == theirs).astype(F32).astype(BF16)
        lift_ref[peer * lanes : (peer + 1) * lanes, :] = mm(theirs, cols, TN).astype(BF16)


def corner_part(got, lift, cases, lanes):
    peers = got.shape[0]
    corners = jnp.concatenate([got[p, :cases, :] for p in range(peers)], axis=1)
    product = mm(stacked(corners), lift[...])
    return stacked(folded(product[:, :lanes]) + product[:cases, lanes:])


def begin_kernel(got, lift, corner, pick, loads, inv, field_ref, *send_refs):
    cases, unknowns = loads.shape
    back = corner_part(got, lift, cases, corner.shape[1])
    width = unknowns // 4
    for side in range(4):
        cols = slice(side * width, (side + 1) * width)
        added = folded(mm(back, corner[cols, :], NT))
        field_ref[:, cols] = stacked(loads[:, cols].astype(F32) * inv[:, cols] + added)
    for pair in range(2):
        cols = slice(2 * pair * width, 2 * (pair + 1) * width)
        sent = folded(mm(field_ref[...], pick[:, cols]))
        send_refs[2 * pair][...] = sent[:, :width]
        send_refs[2 * pair + 1][...] = sent[:, width:]


def lifted_kernel(
    got, lift, leave, ahead, inv_sent, from0, from1, from2, from3, back_ref, *send_refs
):
    cases = ahead.shape[0]
    back = corner_part(got, lift, cases, leave.shape[0])
    back_ref[...] = back
    width = ahead.shape[1] // 4
    for side, came in enumerate((from0, from1, from2, from3)):
        cols = slice(side * width, (side + 1) * width)
        value = ahead[:, cols] - came[...] * inv_sent[:, cols]
        send_refs[side][...] = value + folded(mm(back, leave[:, cols]))


def gram_slot(row, col):
    if row < 0:
        return 0 if col == 0 else gram_slot(0, col - 1)
    return col * (col + 1) // 2 + row + 1


def put(total, slot, value):
    lane = lax.broadcasted_iota(jnp.int32, total.shape, 1)
    return jnp.where(lane == slot, value, total)


def product(first, second):
    return jnp.sum(first * second, axis=1, keepdims=True)


def first_local_kernel(
    field, matrix, corner, pick, inv, loads,
    field_ref, acc_ref, local_ref, local_corner_ref, ahead_ref,
    leave_ref, corner_matrix_ref, inv_sent_ref,
):
    cases, unknowns = loads.shape
    local = folded(mm(field[...], matrix[...]))
    local_ref[...] = local
    local_corner_ref[...] = folded(mm(stacked(local), corner[...]))
    value = field[:cases, :].astype(F32) + field[cases:, :].astype(F32)
    field_ref[...] = value
    total = jnp.zeros(acc_ref.shape, F32)
    acc_ref[...] = put(total, gram_slot(-1, 0), product(value, loads[...].astype(F32)))
    scale = jnp.broadcast_to(inv[...], (8, unknowns))
    high = scale.astype(BF16).astype(F32)
    middle = (scale - high).astype(BF16).astype(F32)
    pieces = jnp.concatenate(
        [high, middle, scale - high - middle, jnp.zeros_like(scale)], axis=0
    ).astype(BF16)
    left = jnp.concatenate([stacked(local * inv[...]), pieces], axis=0)
    wide = unknowns // 4
    for start in range(0, unknowns, wide):
        cols = slice(start, start + wide)
        picked = mm(left, pick[:, cols])
        ahead_ref[:, cols] = folded(picked[: 2 * cases])
        parts = picked[2 * cases :]
        inv_sent_ref[:, cols] = parts[0:1] + parts[8:9] + parts[16:17]
        leave_ref[:, cols] = mm(corner[...], pick[:, cols], TN).astype(BF16)
        corner_matrix_ref[:, cols] = mm(corner[...], matrix[:, cols], TN).astype(BF16)


def local_kernel(*refs, step):
    from0, from1, from2, from3, back, before, local_before = refs[:7]
    matrix, corner, corner_matrix, pick, inv, loads, acc = refs[7:14]
    images = refs[14 : 13 + step]
    outs = refs[13 + step : -2]
    joined, scaled = refs[-2:]
    last = step == ITERS - 1
    cases, unknowns = loads.shape
    image_ref, field_ref, acc_ref = outs[:3]
    width = from0.shape[1]
    for side, came in enumerate((from0, from1, from2, from3)):
        joined[:, side * width : (side + 1) * width] = stacked(came[...])
    chunk = 512
    for start in range(0, unknowns, chunk):
        cols = slice(start, start + chunk)
        image = local_before[:, cols] - folded(mm(joined[...], pick[cols, :], NT))
        image_ref[:, cols] = image
        scaled[:, cols] = stacked(image * inv[:, cols])
    added = folded(mm(back[...], corner[...], NT))
    value = scaled[:cases, :].astype(F32) + scaled[cases:, :].astype(F32) + added
    field_ref[...] = value
    local = folded(mm(scaled[...], matrix[...])) + folded(mm(back[...], corner_matrix[...]))
    total = acc[...]
    for row in range(step):
        image = image_ref if row == step - 1 else images[row]
        total = put(total, gram_slot(row, step), product(value, image[...]))
    total = put(total, gram_slot(step - 1, step - 1), product(before[...], image_ref[...]))
    if last:
        total = put(total, gram_slot(step, step), product(value, local))
    else:
        local_ref, local_corner_ref, ahead_ref = outs[3:]
        local_ref[...] = local
        local_corner_ref[...] = folded(mm(stacked(local), corner[...]))
        scaled[...] = stacked(local * inv[...])
        half = unknowns // 2
        for start in (0, half):
            cols = slice(start, start + half)
            ahead_ref[:, cols] = folded(mm(scaled[...], pick[:, cols]))
    acc_ref[...] = total


def corner_kernel(from0, from1, from2, from3, leave, local_corner, send_ref):
    width = from0.shape[1]
    total = local_corner[...]
    for side, came in enumerate((from0, from1, from2, from3)):
        cols = slice(side * width, (side + 1) * width)
        total = total - folded(mm(stacked(came[...]), leave[:, cols], NT))
    for peer in range(send_ref.shape[0]):
        send_ref[peer] = total


def gram_kernel(acc, sent0, from0, sent2, from2, send_ref):
    total = acc[...]
    lane = lax.broadcasted_iota(jnp.int32, total.shape, 1)
    pairs = sent0[...] * from0[...] + sent2[...] * from2[...]
    coupled = 2.0 * jnp.sum(pairs, axis=1, keepdims=True)
    slot = gram_slot(ITERS - 1, ITERS - 1)
    total = jnp.where(lane == slot, total - coupled, total).T
    packed = jnp.concatenate([total[:GRAM_ROWS], total[GRAM_ROWS : 2 * GRAM_ROWS]], axis=1)
    for peer in range(send_ref.shape[0]):
        send_ref[peer] = packed


def tree_sum(parts):
    while len(parts) > 1:
        parts = [a + b for a, b in zip(parts[::2], parts[1::2])] + parts[len(parts) & ~1 :]
    return parts[0]


def relay_kernel(got, send_ref):
    total = tree_sum([got[p] for p in range(got.shape[0])])
    for peer in range(send_ref.shape[0]):
        send_ref[peer] = total


def solve_kernel(got, *refs):
    fields = refs[:ITERS]
    out_ref, fault_ref = refs[ITERS:]
    total = tree_sum([got[p] for p in range(got.shape[0])])
    cases = out_ref.shape[0]

    def entry(row, col):
        slot = gram_slot(row, col)
        half, at = divmod(slot, GRAM_ROWS)
        return total[at : at + 1, half * cases : (half + 1) * cases]

    n = ITERS
    scale = [lax.rsqrt(entry(k, k)) for k in range(n)]
    rhs = [entry(-1, k) * scale[k] for k in range(n)]
    lower, pivots, solved = {}, [], []
    fault = jnp.zeros_like(rhs[0])
    for k in range(n):
        for j in range(k):
            value = (entry(j, k) * scale[j]) * scale[k]
            for m in range(j):
                value = value - (lower[k, m] * pivots[m]) * lower[j, m]
            lower[k, j] = value / pivots[j]
        pivot = jnp.ones_like(rhs[0])
        value = rhs[k]
        for m in range(k):
            pivot = pivot - (lower[k, m] * pivots[m]) * lower[k, m]
            value = value - lower[k, m] * solved[m]
        pivots.append(pivot)
        solved.append(value)
        good = (pivot > PIVOT_FLOOR) & (scale[k] > 0.0) & (scale[k] < 1e30)
        fault = jnp.maximum(fault, jnp.where(good, 0.0, 1.0))
    parts = [solved[k] * solved[k] / pivots[k] for k in range(n)]
    noise = tree_sum([parts[k] / (pivots[k] * pivots[k]) for k in range(n)])
    good = noise < (NOISE_BOUND / ROUNDING) ** 2 * tree_sum(parts)
    fault = jnp.maximum(fault, jnp.where(good, 0.0, 1.0))
    coeffs = [solved[k] / pivots[k] for k in range(n)]
    for k in reversed(range(n)):
        for m in range(k + 1, n):
            coeffs[k] = coeffs[k] - lower[m, k] * coeffs[m]
    coeffs = [coeffs[k] * scale[k] for k in range(n)]
    for k in range(n):
        good = jnp.abs(coeffs[k]) < 1e37
        fault = jnp.maximum(fault, jnp.where(good, 0.0, 1.0))
    fault_ref[0, 0] = jnp.max(fault)
    spread = jnp.concatenate(coeffs + [jnp.zeros_like(coeffs[0])] * (8 - n), axis=0)
    spread = jnp.concatenate([spread, jnp.zeros_like(spread)], axis=1).T[:cases]
    width = out_ref.shape[1] // 4
    for part in range(4):
        cols = slice(part * width, (part + 1) * width)
        value = spread[:, 0:1] * fields[0][:, cols]
        for k in range(1, n):
            value = value + spread[:, k : k + 1] * fields[k][:, cols]
        out_ref[:, cols] = value.astype(BF16)


def shifted(value, axis, shift, wrap):
    count = lax.axis_size(axis)
    pairs = [(i, (i + shift) % count) for i in range(count) if wrap or 0 <= i + shift < count]
    return lax.ppermute(value, axis, pairs)


def exchange(send, axis, groups=None):
    return lax.all_to_all(send, axis, 0, 0, axis_index_groups=groups)


def sum_groups(span, chord, inner):
    outer = span // inner
    first = [
        [(o * inner + i) * chord + c for o in range(outer) for c in range(chord)]
        for i in range(inner)
    ]
    second = [[o * inner + i for i in range(inner)] for o in range(outer)]
    return first, second


def shards(schur, loads, interface_rows, edge_rows, corner_rows, corner_map, coarse_inverse):
    originals = (
        schur, loads, interface_rows, edge_rows, corner_rows, corner_map, coarse_inverse
    )
    span, chord = lax.axis_size("span"), lax.axis_size("chord")
    matrix, rhs, block = schur[0, 0], loads[0, 0], coarse_inverse[0]
    unknowns = matrix.shape[0]
    cases = rhs.shape[0]
    rows, counts = interface_rows[0, 0], edge_rows[0, 0]
    width = rows.shape[1]
    lanes = corner_rows.shape[2]
    own, total = block.shape
    slots = corner_map[0]

    tile = 128
    turn = lax.rem(total - lax.axis_index("chord") * own, total).astype(jnp.int32).reshape(1)
    pick, corner, inv, send = pl.pallas_call(
        setup_kernel,
        in_specs=[pl.BlockSpec(memory_space=pltpu.SMEM)] * 2
        + [pl.BlockSpec(memory_space=pl.ANY)]
        + [pl.BlockSpec(memory_space=pltpu.VMEM)] * 5,
        out_shape=(
            shape((unknowns, unknowns), BF16),
            shape((unknowns, lanes), BF16),
            shape((1, unknowns), F32),
            shape((chord, cases + own * coarse_parts(own, chord, lanes) + 8, lanes), F32),
        ),
        scratch_shapes=[
            pltpu.VMEM((unknowns // tile, tile, tile), BF16),
            pltpu.SemaphoreType.DMA((unknowns // tile,)),
        ],
        compiler_params=pltpu.CompilerParams(vmem_limit_bytes=28 * 2**20),
    )(counts, turn, matrix, rhs, rows, corner_rows[0], slots, block)
    got = exchange(send, "chord")
    lift = call(
        functools.partial(lift_kernel, cases=cases, own=own),
        shape((chord * lanes, 2 * lanes), BF16),
    )(slots, got)

    full = shape((cases, unknowns), F32)
    edges = (shape((cases, width), F32),) * 4
    table = shape((cases, 128), F32)
    corners = shape((cases, lanes), F32)
    doubled = shape((2 * cases, unknowns), BF16)
    fields, images = [], []
    for step in range(ITERS):
        last = step == ITERS - 1
        if step == 0:
            first, *sends = call(begin_kernel, (doubled, *edges))(
                got, lift, corner, pick, rhs, inv
            )
        else:
            back, *sends = call(lifted_kernel, (shape((2 * cases, lanes), BF16), *edges))(
                got, lift, leave, ahead, inv_sent, *came
            )
        earlier = came if step else ()
        came = [
            shifted(sends[1], "span", 1, False),
            None if last else shifted(sends[0], "span", -1, False),
            shifted(sends[3], "chord", 1, True),
            None if last else shifted(sends[2], "chord", -1, True),
        ]
        if step == 0:
            field, acc, local, local_corner, ahead, leave, corner_matrix, inv_sent = call(
                first_local_kernel,
                (
                    full, table, full, corners, full,
                    shape((lanes, unknowns), BF16),
                    shape((lanes, unknowns), BF16),
                    shape((1, unknowns), F32),
                ),
                flops=10**9,
            )(first, matrix, corner, pick, inv, rhs)
        else:
            image, field, acc, *rest = call(
                functools.partial(local_kernel, step=step),
                (full, full, table) + (() if last else (full, corners, full)),
                scratch=[pltpu.VMEM(doubled.shape, BF16)] * 2,
                flops=10**9,
            )(
                *earlier, back, fields[-1], local,
                matrix, corner, corner_matrix, pick, inv, rhs, acc, *images,
            )
            images.append(image)
            if not last:
                local, local_corner, ahead = rest
        fields.append(field)
        if not last:
            send = call(corner_kernel, shape((chord, cases, lanes), F32))(
                *came, leave, local_corner
            )
            got = exchange(send, "chord")

    inner = 16 if span % 16 == 0 else span
    first, second = sum_groups(span, chord, inner)
    send = call(gram_kernel, shape((len(first[0]), GRAM_ROWS, 128), F32))(
        acc, sends[0], came[0], sends[2], came[2]
    )
    got = exchange(send, ("span", "chord"), first)
    send = call(relay_kernel, shape((inner, GRAM_ROWS, 128), F32))(got)
    got = exchange(send, "span", second)
    answer, fault = pl.pallas_call(
        solve_kernel,
        out_shape=(shape((cases, unknowns), BF16), shape((1, 1), F32)),
        out_specs=(
            pl.BlockSpec(memory_space=pltpu.VMEM),
            pl.BlockSpec(memory_space=pltpu.SMEM),
        ),
        compiler_params=pltpu.CompilerParams(vmem_limit_bytes=28 * 2**20),
    )(got, *fields)
    answer = lax.cond(
        fault[0, 0] > 0.0,
        lambda answer, *arrays: plain_recurrence(*arrays),
        lambda answer, *arrays: answer,
        answer,
        *originals,
    )
    return answer[None, None]


def solution(mesh):
    return jax.shard_map(
        shards,
        mesh=mesh,
        in_specs=(
            P("span", "chord", None, None),
            P("span", "chord", None, None),
            P("span", "chord", None, None),
            P("span", "chord", None),
            P("span", "chord", None),
            P("span", "chord", None),
            P("span", "chord", None),
        ),
        out_specs=P("span", "chord", None, None),
        check_vma=False,
    )
```

```python
import functools

import jax
import jax.numpy as jnp
from jax import lax
from jax.experimental import pallas as pl
from jax.experimental.pallas import tpu as pltpu
from jax.sharding import PartitionSpec as P

ITERS = 5
F32 = jnp.float32
BF16 = jnp.bfloat16
PIVOT_FLOOR = 2e-5
NOISE_BOUND = 2.5e-4
ROUNDING = 1.2e-7
GRAM_ROWS = 8


def with_halo(block, sides, width):
    for axis, dim in sides:
        count = lax.axis_size(axis)
        forward = [(i, i + 1) for i in range(count - 1)]
        backward = [(target, source) for source, target in forward]
        low = lax.ppermute(
            lax.slice_in_dim(block, block.shape[dim] - width, None, axis=dim), axis, forward
        )
        high = lax.ppermute(lax.slice_in_dim(block, 0, width, axis=dim), axis, backward)
        block = jnp.concatenate([low, block, high], axis=dim)
    return block


def case_sum(first, second):
    return lax.psum(jnp.sum(first * second, axis=1), ("span", "chord"))


def plain_recurrence(
    schur, loads, interface_rows, edge_rows, corner_rows, corner_map, coarse_inverse
):
    matrix = schur[0, 0]
    rows = interface_rows[0, 0]
    counts = edge_rows[0, 0]
    corners = corner_rows[0, 0]
    block = coarse_inverse[0]
    width = rows.shape[1]
    unknowns = matrix.shape[0]
    total_rows = block.shape[1]
    live = (jnp.arange(width, dtype=jnp.int32)[None, :] < counts[:, None]).astype(BF16)
    flat_rows = rows.reshape(-1)
    inv_diag = 1.0 / jnp.diagonal(matrix).astype(F32)
    onehot = (
        corner_map[0, 0][:, None] == jnp.arange(total_rows, dtype=jnp.int32)[None, :]
    ).astype(F32)
    highest = lax.Precision.HIGHEST

    def precondition(resid):
        term = jnp.dot(resid[:, corners], onehot, precision=highest)
        summed = lax.psum(term, "chord")
        own_rows = jnp.dot(summed, block.T, precision=highest)
        lifted = lax.all_gather(own_rows, "chord", axis=1, tiled=True)
        back = jnp.dot(lifted, onehot.T, precision=highest)
        return (resid * inv_diag[None, :]).at[:, corners].add(back)

    def apply_operator(direction):
        rounded = direction.astype(BF16)
        picks = [rounded[:, rows[side]] * live[side][None, :] for side in range(4)]
        span_ext = with_halo(jnp.stack([picks[0], picks[1]]), (("span", 0),), 1)
        chord_ext = with_halo(jnp.stack([picks[2], picks[3]]), (("chord", 0),), 1)
        local = jnp.dot(rounded, matrix, preferred_element_type=F32)
        arrived = jnp.concatenate([span_ext[0], span_ext[3], chord_ext[0], chord_ext[3]], axis=1)
        coupled = (
            jnp.zeros((direction.shape[0], unknowns), F32)
            .at[:, flat_rows]
            .add(arrived.astype(F32))
        )
        return local - coupled

    resid = loads[0, 0].astype(F32)
    result = jnp.zeros_like(resid)
    direction = precondition(resid)
    norm_now = case_sum(resid, direction)

    def step(_, carry):
        result, resid, direction, norm_now = carry
        image = apply_operator(direction)
        alpha = norm_now / case_sum(direction, image)
        result = result + alpha[:, None] * direction
        resid = resid - alpha[:, None] * image
        precond = precondition(resid)
        norm_next = case_sum(resid, precond)
        direction = precond + (norm_next / norm_now)[:, None] * direction
        return result, resid, direction, norm_next

    result, resid, direction, norm_now = lax.fori_loop(
        0, ITERS - 1, step, (result, resid, direction, norm_now)
    )
    alpha = norm_now / case_sum(direction, apply_operator(direction))
    return (result + alpha[:, None] * direction).astype(BF16)


NN = (((1,), (0,)), ((), ()))
NT = (((1,), (1,)), ((), ()))
TN = (((0,), (0,)), ((), ()))


def mm(first, second, dims=NN):
    return lax.dot_general(first, second, dims, preferred_element_type=F32)


def halves(value):
    high = value.astype(BF16)
    return high, (value - high.astype(F32)).astype(BF16)


def stacked(value):
    return jnp.concatenate(halves(value), axis=0)


def folded(value):
    half = value.shape[0] // 2
    return value[:half] + value[half:]


def call(body, outs, scratch=(), limit=28, flops=10**8):
    return pl.pallas_call(
        body,
        out_shape=outs,
        scratch_shapes=list(scratch),
        compiler_params=pltpu.CompilerParams(vmem_limit_bytes=limit * 2**20),
        cost_estimate=pl.CostEstimate(flops=flops, bytes_accessed=10**6, transcendentals=0),
    )


def shape(dims, dtype):
    return jax.ShapeDtypeStruct(dims, dtype)


def setup_kernel(
    counts, turn_ref, schur, loads, rows, corners, slots, coarse,
    pick_ref, corner_ref, inv_ref, send_ref, blocks, sems,
):
    unknowns = loads.shape[1]
    lanes = corners.shape[1]
    tile = blocks.shape[1]
    copies = []
    for part in range(unknowns // tile):
        span = pl.ds(part * tile, tile)
        copy = pltpu.make_async_copy(schur.at[span, span], blocks.at[part], sems.at[part])
        copy.start()
        copies.append(copy)

    sides, width = rows.shape
    lane = lax.broadcasted_iota(jnp.int32, (1, width), 1)
    live = [jnp.where(lane < counts[side], rows[side : side + 1, :], -1) for side in range(sides)]

    def build(step, _):
        start = pl.multiple_of(step * tile, tile)
        index = lax.broadcasted_iota(jnp.int32, (tile, width), 0) + start
        for side in range(sides):
            cols = slice(side * width, (side + 1) * width)
            pick_ref[pl.ds(start, tile), cols] = (index == live[side]).astype(F32).astype(BF16)
        index = lax.broadcasted_iota(jnp.int32, (tile, lanes), 0) + start
        corner_ref[pl.ds(start, tile), :] = (index == corners[...]).astype(F32).astype(BF16)
        return 0

    lax.fori_loop(0, unknowns // tile, build, 0)
    eye = lax.broadcasted_iota(jnp.int32, (tile, tile), 0) == lax.broadcasted_iota(
        jnp.int32, (tile, tile), 1
    )
    for part, copy in enumerate(copies):
        copy.wait()
        block = blocks[part].astype(F32)
        diag = jnp.sum(jnp.where(eye, block, 0.0), axis=0, keepdims=True)
        inv_ref[:, part * tile : (part + 1) * tile] = 1.0 / diag
    picked = mm(loads[...], corner_ref[...])
    cases = picked.shape[0]
    own, total = coarse.shape
    parts = (send_ref.shape[1] - cases - 8) // own
    turned = pltpu.roll(coarse[...], turn_ref[0], 1)
    for peer in range(send_ref.shape[0]):
        send_ref[peer, :cases, :] = picked
        for part in range(parts):
            send_ref[peer, cases + part * own : cases + (part + 1) * own, :] = turned[
                :, part * lanes : (part + 1) * lanes
            ]
        send_ref[peer, cases + own * parts :, :] = jnp.broadcast_to(
            slots[...].astype(F32), (8, lanes)
        )


def coarse_parts(own, peers, lanes):
    return -(-own * (peers // 2 + 1) // lanes)


def lift_kernel(slots, got, lift_ref, *, cases, own):
    peers, _, lanes = got.shape
    total = own * peers
    parts = coarse_parts(own, peers, lanes)
    index = lax.broadcasted_iota(jnp.int32, (total, lanes), 0)
    mine = (index == slots[...]).astype(F32).astype(BF16)
    lane = lax.broadcasted_iota(jnp.int32, (own, total), 1)
    reach = own * (peers // 2)
    weight = jnp.where((lane < own) | (lane >= reach), 0.5, 1.0)
    weight = jnp.where(lane < reach + own, weight, 0.0)
    rows = []
    for p in range(peers):
        pieces = [got[p, cases + q * own : cases + (q + 1) * own, :] for q in range(parts)]
        pieces += [jnp.zeros((own, lanes), F32)] * (total // lanes - parts)
        row = jnp.concatenate(pieces, axis=1) * weight
        rows.append(pltpu.roll(row, p * own, 1) if p else row)
    half = jnp.concatenate(rows, axis=0)
    inverse = half + half.T
    high = inverse.astype(BF16)
    rest = inverse - high.astype(F32)
    middle, low = halves(rest)
    cols = (mm(high, mine) + mm(middle, mine)) + mm(low, mine)
    cols = jnp.concatenate(halves(cols), axis=1)
    base = cases + own * parts
    for peer in range(peers):
        theirs = got[peer, base : base + 1, :].astype(jnp.int32)
        theirs = (index == theirs).astype(F32).astype(BF16)
        lift_ref[peer * lanes : (peer + 1) * lanes, :] = mm(theirs, cols, TN).astype(BF16)


def corner_part(got, lift, cases, lanes):
    peers = got.shape[0]
    corners = jnp.concatenate([got[p, :cases, :] for p in range(peers)], axis=1)
    product = mm(stacked(corners), lift[...])
    return stacked(folded(product[:, :lanes]) + product[:cases, lanes:])


def begin_kernel(got, lift, corner, pick, loads, inv, field_ref, *send_refs):
    cases, unknowns = loads.shape
    back = corner_part(got, lift, cases, corner.shape[1])
    width = unknowns // 4
    for side in range(4):
        cols = slice(side * width, (side + 1) * width)
        added = folded(mm(back, corner[cols, :], NT))
        field_ref[:, cols] = stacked(loads[:, cols].astype(F32) * inv[:, cols] + added)
    for pair in range(2):
        cols = slice(2 * pair * width, 2 * (pair + 1) * width)
        sent = folded(mm(field_ref[...], pick[:, cols]))
        send_refs[2 * pair][...] = sent[:, :width]
        send_refs[2 * pair + 1][...] = sent[:, width:]


def lifted_kernel(
    got, lift, leave, ahead, inv_sent, from0, from1, from2, from3, back_ref, *send_refs
):
    cases = ahead.shape[0]
    back = corner_part(got, lift, cases, leave.shape[0])
    back_ref[...] = back
    width = ahead.shape[1] // 4
    for side, came in enumerate((from0, from1, from2, from3)):
        cols = slice(side * width, (side + 1) * width)
        value = ahead[:, cols] - came[...] * inv_sent[:, cols]
        send_refs[side][...] = value + folded(mm(back, leave[:, cols]))


def gram_slot(row, col):
    if row < 0:
        return 0 if col == 0 else gram_slot(0, col - 1)
    return col * (col + 1) // 2 + row + 1


def put(total, slot, value):
    lane = lax.broadcasted_iota(jnp.int32, total.shape, 1)
    return jnp.where(lane == slot, value, total)


def product(first, second):
    return jnp.sum(first * second, axis=1, keepdims=True)


def first_local_kernel(
    field, matrix, corner, pick, inv, loads,
    field_ref, acc_ref, local_ref, local_corner_ref, ahead_ref,
    leave_ref, corner_matrix_ref, inv_sent_ref,
):
    cases, unknowns = loads.shape
    local = folded(mm(field[...], matrix[...]))
    local_ref[...] = local
    local_corner_ref[...] = folded(mm(stacked(local), corner[...]))
    value = field[:cases, :].astype(F32) + field[cases:, :].astype(F32)
    field_ref[...] = value
    total = jnp.zeros(acc_ref.shape, F32)
    acc_ref[...] = put(total, gram_slot(-1, 0), product(value, loads[...].astype(F32)))
    scale = jnp.broadcast_to(inv[...], (8, unknowns))
    high = scale.astype(BF16).astype(F32)
    middle = (scale - high).astype(BF16).astype(F32)
    pieces = jnp.concatenate(
        [high, middle, scale - high - middle, jnp.zeros_like(scale)], axis=0
    ).astype(BF16)
    left = jnp.concatenate([stacked(local * inv[...]), pieces], axis=0)
    wide = unknowns // 4
    for start in range(0, unknowns, wide):
        cols = slice(start, start + wide)
        picked = mm(left, pick[:, cols])
        ahead_ref[:, cols] = folded(picked[: 2 * cases])
        parts = picked[2 * cases :]
        inv_sent_ref[:, cols] = parts[0:1] + parts[8:9] + parts[16:17]
        leave_ref[:, cols] = mm(corner[...], pick[:, cols], TN).astype(BF16)
        corner_matrix_ref[:, cols] = mm(corner[...], matrix[:, cols], TN).astype(BF16)


def local_kernel(*refs, step):
    from0, from1, from2, from3, back, before, local_before = refs[:7]
    matrix, corner, corner_matrix, pick, inv, loads, acc = refs[7:14]
    images = refs[14 : 13 + step]
    outs = refs[13 + step : -2]
    joined, scaled = refs[-2:]
    last = step == ITERS - 1
    cases, unknowns = loads.shape
    image_ref, field_ref, acc_ref = outs[:3]
    width = from0.shape[1]
    for side, came in enumerate((from0, from1, from2, from3)):
        joined[:, side * width : (side + 1) * width] = stacked(came[...])
    chunk = 512
    for start in range(0, unknowns, chunk):
        cols = slice(start, start + chunk)
        image = local_before[:, cols] - folded(mm(joined[...], pick[cols, :], NT))
        image_ref[:, cols] = image
        scaled[:, cols] = stacked(image * inv[:, cols])
    added = folded(mm(back[...], corner[...], NT))
    value = scaled[:cases, :].astype(F32) + scaled[cases:, :].astype(F32) + added
    field_ref[...] = value
    local = folded(mm(scaled[...], matrix[...])) + folded(mm(back[...], corner_matrix[...]))
    total = acc[...]
    for row in range(step):
        image = image_ref if row == step - 1 else images[row]
        total = put(total, gram_slot(row, step), product(value, image[...]))
    total = put(total, gram_slot(step - 1, step - 1), product(before[...], image_ref[...]))
    if last:
        total = put(total, gram_slot(step, step), product(value, local))
    else:
        local_ref, local_corner_ref, ahead_ref = outs[3:]
        local_ref[...] = local
        local_corner_ref[...] = folded(mm(stacked(local), corner[...]))
        scaled[...] = stacked(local * inv[...])
        half = unknowns // 2
        for start in (0, half):
            cols = slice(start, start + half)
            ahead_ref[:, cols] = folded(mm(scaled[...], pick[:, cols]))
    acc_ref[...] = total


def corner_kernel(from0, from1, from2, from3, leave, local_corner, send_ref):
    width = from0.shape[1]
    total = local_corner[...]
    for side, came in enumerate((from0, from1, from2, from3)):
        cols = slice(side * width, (side + 1) * width)
        total = total - folded(mm(stacked(came[...]), leave[:, cols], NT))
    for peer in range(send_ref.shape[0]):
        send_ref[peer] = total


def gram_kernel(acc, sent0, from0, sent2, from2, send_ref):
    total = acc[...]
    lane = lax.broadcasted_iota(jnp.int32, total.shape, 1)
    pairs = sent0[...] * from0[...] + sent2[...] * from2[...]
    coupled = 2.0 * jnp.sum(pairs, axis=1, keepdims=True)
    slot = gram_slot(ITERS - 1, ITERS - 1)
    total = jnp.where(lane == slot, total - coupled, total).T
    packed = jnp.concatenate([total[:GRAM_ROWS], total[GRAM_ROWS : 2 * GRAM_ROWS]], axis=1)
    for peer in range(send_ref.shape[0]):
        send_ref[peer] = packed


def tree_sum(parts):
    while len(parts) > 1:
        parts = [a + b for a, b in zip(parts[::2], parts[1::2])] + parts[len(parts) & ~1 :]
    return parts[0]


def relay_kernel(got, send_ref):
    total = tree_sum([got[p] for p in range(got.shape[0])])
    for peer in range(send_ref.shape[0]):
        send_ref[peer] = total


def solve_kernel(got, coeff_ref, fault_ref):
    total = tree_sum([got[p] for p in range(got.shape[0])])
    cases = coeff_ref.shape[0]

    def entry(row, col):
        slot = gram_slot(row, col)
        half, at = divmod(slot, GRAM_ROWS)
        return total[at : at + 1, half * cases : (half + 1) * cases]

    n = ITERS
    scale = [lax.rsqrt(entry(k, k)) for k in range(n)]
    rhs = [entry(-1, k) * scale[k] for k in range(n)]
    lower, pivots, solved = {}, [], []
    fault = jnp.zeros_like(rhs[0])
    for k in range(n):
        for j in range(k):
            value = (entry(j, k) * scale[j]) * scale[k]
            for m in range(j):
                value = value - (lower[k, m] * pivots[m]) * lower[j, m]
            lower[k, j] = value / pivots[j]
        pivot = jnp.ones_like(rhs[0])
        value = rhs[k]
        for m in range(k):
            pivot = pivot - (lower[k, m] * pivots[m]) * lower[k, m]
            value = value - lower[k, m] * solved[m]
        pivots.append(pivot)
        solved.append(value)
        good = (pivot > PIVOT_FLOOR) & (scale[k] > 0.0) & (scale[k] < 1e30)
        fault = jnp.maximum(fault, jnp.where(good, 0.0, 1.0))
    parts = [solved[k] * solved[k] / pivots[k] for k in range(n)]
    noise = tree_sum([parts[k] / (pivots[k] * pivots[k]) for k in range(n)])
    good = noise < (NOISE_BOUND / ROUNDING) ** 2 * tree_sum(parts)
    fault = jnp.maximum(fault, jnp.where(good, 0.0, 1.0))
    coeffs = [solved[k] / pivots[k] for k in range(n)]
    for k in reversed(range(n)):
        for m in range(k + 1, n):
            coeffs[k] = coeffs[k] - lower[m, k] * coeffs[m]
    coeffs = [coeffs[k] * scale[k] for k in range(n)]
    for k in range(n):
        good = jnp.abs(coeffs[k]) < 1e37
        fault = jnp.maximum(fault, jnp.where(good, 0.0, 1.0))
    fault_ref[0, 0] = jnp.max(fault)
    spread = jnp.concatenate(coeffs + [jnp.zeros_like(coeffs[0])] * (8 - n), axis=0)
    spread = jnp.concatenate([spread, jnp.zeros_like(spread)], axis=1).T[:cases]
    coeff_ref[...] = jnp.concatenate([spread, jnp.zeros((cases, 120), F32)], axis=1)


def combine_kernel(coeff, *refs):
    fields, out_ref = refs[:-1], refs[-1]
    n = ITERS
    spread = coeff[...]
    width = out_ref.shape[1] // 4
    for part in range(4):
        cols = slice(part * width, (part + 1) * width)
        value = spread[:, 0:1] * fields[0][:, cols]
        for k in range(1, n):
            value = value + spread[:, k : k + 1] * fields[k][:, cols]
        out_ref[:, cols] = value.astype(BF16)


def shifted(value, axis, shift, wrap):
    count = lax.axis_size(axis)
    pairs = [(i, (i + shift) % count) for i in range(count) if wrap or 0 <= i + shift < count]
    return lax.ppermute(value, axis, pairs)


def exchange(send, axis, groups=None):
    return lax.all_to_all(send, axis, 0, 0, axis_index_groups=groups)


def sum_groups(span, chord, inner):
    outer = span // inner
    first = [
        [(o * inner + i) * chord + c for o in range(outer) for c in range(chord)]
        for i in range(inner)
    ]
    second = [[o * inner + i for i in range(inner)] for o in range(outer)]
    return first, second


def shards(schur, loads, interface_rows, edge_rows, corner_rows, corner_map, coarse_inverse):
    originals = (
        schur, loads, interface_rows, edge_rows, corner_rows, corner_map, coarse_inverse
    )
    span, chord = lax.axis_size("span"), lax.axis_size("chord")
    matrix, rhs, block = schur[0, 0], loads[0, 0], coarse_inverse[0]
    unknowns = matrix.shape[0]
    cases = rhs.shape[0]
    rows, counts = interface_rows[0, 0], edge_rows[0, 0]
    width = rows.shape[1]
    lanes = corner_rows.shape[2]
    own, total = block.shape
    slots = corner_map[0]

    tile = 128
    turn = lax.rem(total - lax.axis_index("chord") * own, total).astype(jnp.int32).reshape(1)
    pick, corner, inv, send = pl.pallas_call(
        setup_kernel,
        in_specs=[pl.BlockSpec(memory_space=pltpu.SMEM)] * 2
        + [pl.BlockSpec(memory_space=pl.ANY)]
        + [pl.BlockSpec(memory_space=pltpu.VMEM)] * 5,
        out_shape=(
            shape((unknowns, unknowns), BF16),
            shape((unknowns, lanes), BF16),
            shape((1, unknowns), F32),
            shape((chord, cases + own * coarse_parts(own, chord, lanes) + 8, lanes), F32),
        ),
        scratch_shapes=[
            pltpu.VMEM((unknowns // tile, tile, tile), BF16),
            pltpu.SemaphoreType.DMA((unknowns // tile,)),
        ],
        compiler_params=pltpu.CompilerParams(vmem_limit_bytes=28 * 2**20),
    )(counts, turn, matrix, rhs, rows, corner_rows[0], slots, block)
    got = exchange(send, "chord")
    lift = call(
        functools.partial(lift_kernel, cases=cases, own=own),
        shape((chord * lanes, 2 * lanes), BF16),
    )(slots, got)

    full = shape((cases, unknowns), F32)
    edges = (shape((cases, width), F32),) * 4
    table = shape((cases, 128), F32)
    corners = shape((cases, lanes), F32)
    doubled = shape((2 * cases, unknowns), BF16)
    fields, images = [], []
    for step in range(ITERS):
        last = step == ITERS - 1
        if step == 0:
            first, *sends = call(begin_kernel, (doubled, *edges))(
                got, lift, corner, pick, rhs, inv
            )
        else:
            back, *sends = call(lifted_kernel, (shape((2 * cases, lanes), BF16), *edges))(
                got, lift, leave, ahead, inv_sent, *came
            )
        earlier = came if step else ()
        came = [
            shifted(sends[1], "span", 1, False),
            None if last else shifted(sends[0], "span", -1, False),
            shifted(sends[3], "chord", 1, True),
            None if last else shifted(sends[2], "chord", -1, True),
        ]
        if step == 0:
            field, acc, local, local_corner, ahead, leave, corner_matrix, inv_sent = call(
                first_local_kernel,
                (
                    full, table, full, corners, full,
                    shape((lanes, unknowns), BF16),
                    shape((lanes, unknowns), BF16),
                    shape((1, unknowns), F32),
                ),
                flops=10**9,
            )(first, matrix, corner, pick, inv, rhs)
        else:
            image, field, acc, *rest = call(
                functools.partial(local_kernel, step=step),
                (full, full, table) + (() if last else (full, corners, full)),
                scratch=[pltpu.VMEM(doubled.shape, BF16)] * 2,
                flops=10**9,
            )(
                *earlier, back, fields[-1], local,
                matrix, corner, corner_matrix, pick, inv, rhs, acc, *images,
            )
            images.append(image)
            if not last:
                local, local_corner, ahead = rest
        fields.append(field)
        if not last:
            send = call(corner_kernel, shape((chord, cases, lanes), F32))(
                *came, leave, local_corner
            )
            got = exchange(send, "chord")

    inner = 16 if span % 16 == 0 else span
    first, second = sum_groups(span, chord, inner)
    send = call(gram_kernel, shape((len(first[0]), GRAM_ROWS, 128), F32))(
        acc, sends[0], came[0], sends[2], came[2]
    )
    got = exchange(send, ("span", "chord"), first)
    send = call(relay_kernel, shape((inner, GRAM_ROWS, 128), F32))(got)
    got = exchange(send, "span", second)
    coeffs, fault = pl.pallas_call(
        solve_kernel,
        out_shape=(table, shape((1, 1), F32)),
        out_specs=(
            pl.BlockSpec(memory_space=pltpu.VMEM),
            pl.BlockSpec(memory_space=pltpu.SMEM),
        ),
        compiler_params=pltpu.CompilerParams(vmem_limit_bytes=28 * 2**20),
    )(got)
    answer = lax.cond(
        fault[0, 0] > 0.0,
        lambda parts, arrays: plain_recurrence(*arrays),
        lambda parts, arrays: call(combine_kernel, shape((cases, unknowns), BF16))(*parts),
        (coeffs, *fields),
        originals,
    )
    return answer[None, None]


def solution(mesh):
    return jax.shard_map(
        shards,
        mesh=mesh,
        in_specs=(
            P("span", "chord", None, None),
            P("span", "chord", None, None),
            P("span", "chord", None, None),
            P("span", "chord", None),
            P("span", "chord", None),
            P("span", "chord", None),
            P("span", "chord", None),
        ),
        out_specs=P("span", "chord", None, None),
        check_vma=False,
    )
```
